128 devices in a mesh: row: 8 (over x, z_lo), col: 16 (over y, z_hi, core).
Axes of the slice: x: 4, y: 4, z: 4 (z_hi: 2, z_lo: 2; z = z_hi * 2 + z_lo), core: 2. Of those that a mesh axis runs over, the one named last changes fastest.
Arguments:
- attributes: bfloat16 [65536, 128], P(('row', 'col')), may hold values from -6 to 6
- adj_values: bfloat16 [8, 16, 384, 128, 128], P('row', 'col'), may hold values from 0 to 3, as said below
- adj_rows: int32 [8, 16, 384], P('row', 'col'), may hold values from 0 to 63
- adj_cols: int32 [8, 16, 384], P('row', 'col'), may hold values from 0 to 31
- adj_count: int32 [8, 16], P('row', 'col'), may hold values from 1 to 384, as said below
- pair_ids: int32 [512, 4], P(('row', 'col')), may hold values from 0 to 31
- struct_target: bfloat16 [65536, 4, 128], P(('row', 'col')), may hold values from 0 to 1
- w_first: bfloat16 [128, 512], replicated, may hold values from -0.5 to 0.5
- w_rest: bfloat16 [1, 256, 512], replicated, may hold values from -0.375 to 0.375
- layer_bias: float32 [1, 256], replicated, may hold values from -3 to 3
- w_attr: bfloat16 [256, 128], replicated, may hold values from -0.375 to 0.375
- attr_bias: float32 [128], replicated, may hold values from -3 to 3
Outputs:
- anomaly: float32 [65536], P(('row', 'col'))
The draws below stay inside these ranges and needn't reach their ends.
Inputs may be any that keep to these rules, and one draw needn't show every extreme that they name: `adj_count`: every tile has at least one live slot, and some tile has all 384 live in every draw. `adj_values`: nonnegative entries; slots at or past a tile's count are ignored.
All inputs are finite; a program needn't handle non-finite values.
Results may differ from the reference program's by a relative error of at most 0.00075.
Values may be sent and summed in bfloat16 or wider, within the bound.
No kernel may reach another device: no remote copies, remote signals or barrier semaphores. Data moves between devices by JAX's collectives and lax.ppermute only.
A program may use at most 128 MiB of HBM per device.

```python
import math
import jax
import jax.numpy as jnp
from jax import lax

F_IN = 128
HID = 256
BLK = 128
LAYERS = 2
PAIRS = 4
V_DEV = 512
NODES = 65536
BLOCKS_DEV = 4
NODE_BLOCKS = 512
TILE_ROWB = 64
TILE_COLB = 32
K_CAP = 384
N_ROW = 8
N_COL = 16


def draw_adj_values(key, part):
    key = jax.random.fold_in(key, 11)
    key_main = jax.random.fold_in(key, 1)
    col_ramp = 1.0 + 2.0 * jnp.arange(N_COL, dtype=jnp.float32) / max(N_COL - 1, 1)
    uniform_part = jax.random.uniform(key_main, (N_ROW, N_COL, K_CAP, BLK, BLK), jnp.float32)
    return (uniform_part * col_ramp[None, :, None, None, None]).astype(jnp.bfloat16)


def draw_adj_count(key, part):
    key = jax.random.fold_in(key, 23)
    key_shift = jax.random.fold_in(key, 1)
    key_jitter = jax.random.fold_in(key, 2)
    key_spot = jax.random.fold_in(key, 3)
    shifts = jax.random.randint(key_shift, (N_ROW, N_COL), 0, 3)
    base_counts = K_CAP // jnp.power(jnp.int32(2), shifts.astype(jnp.int32))
    jitter = jax.random.randint(key_jitter, (N_ROW, N_COL), 0, K_CAP // 8 + 1)
    counts = jnp.maximum(base_counts - jitter, 1).astype(jnp.int32)
    spot = jax.random.randint(key_spot, (), 0, N_ROW * N_COL)
    flattened = counts.reshape(-1).at[spot].set(K_CAP)
    return flattened.reshape(N_ROW, N_COL).astype(jnp.int32)


def plant(entries, own_key, least, top_value):
    longest = entries.shape.index(max(entries.shape))
    spots = []
    for shift in (0, 1):
        where = [jax.random.randint(jax.random.fold_in(own_key, axis), (), 0, length) for axis, length in enumerate(entries.shape)]
        where[longest] = (where[longest] + shift) % entries.shape[longest]
        spots.append(tuple(where))
    return entries.at[spots[0]].set(least).at[spots[1]].set(top_value)


def block_scale(rng, extent, cuts, smallest, largest):
    def one(axis_at, blocks):
        heights = jax.random.uniform(jax.random.fold_in(jax.random.fold_in(rng, 6), axis_at), (blocks,), jnp.float32, smallest / len(cuts), largest / len(cuts))
        return jnp.repeat(jnp.exp(heights), extent[axis_at] // blocks).reshape((-1,) + (1,) * (len(extent) - axis_at - 1))

    level = one(*cuts[0])
    for cut in cuts[1:]:
        level = level * one(*cut)
    return level


def centred(stream_key, shape, deviation, most, cuts=(), kind=jnp.bfloat16):
    values = deviation * jax.random.normal(stream_key, shape, jnp.float32)
    if cuts:
        values = values * block_scale(stream_key, shape, cuts, -0.22, 0.18)
    return jnp.clip(values, -most, most).astype(kind)


def setup_inputs(seed: int = 0) -> dict:
    splits = jax.random.split(jax.random.key(seed), 13)
    attributes = centred(splits[0], (NODES, F_IN), 1.0, 6.0, ((0, 128),))
    adj_values = draw_adj_values(jax.random.fold_in(splits[12], 71), 0)
    adj_rows = plant(jax.random.randint(splits[2], (N_ROW, N_COL, K_CAP), 0, TILE_ROWB), jax.random.fold_in(splits[2], 1), 0, TILE_ROWB - 1).astype(jnp.int32)
    adj_cols = plant(jax.random.randint(splits[3], (N_ROW, N_COL, K_CAP), 0, TILE_COLB), jax.random.fold_in(splits[3], 1), 0, TILE_COLB - 1).astype(jnp.int32)
    adj_count = draw_adj_count(jax.random.fold_in(splits[12], 71), 0)
    pair_ids = plant(jax.random.randint(splits[5], (NODE_BLOCKS, PAIRS), 0, TILE_COLB), jax.random.fold_in(splits[5], 1), 0, TILE_COLB - 1).astype(jnp.int32)
    struct_target = jnp.clip(1.0 * jax.random.uniform(splits[6], (NODES, PAIRS, BLK), jnp.float32) ** block_scale(splits[6], (NODES, PAIRS, BLK), ((0, 128),), -0.2, 0.2), 0.0, 1.0).astype(jnp.bfloat16)
    w_first = centred(splits[7], (F_IN, 2 * HID), F_IN ** -0.5, 0.5)
    w_rest = centred(splits[8], (LAYERS - 1, HID, 2 * HID), HID ** -0.5, 0.375)
    layer_bias = centred(splits[9], (LAYERS - 1, HID), 0.5, 3.0, (), jnp.float32)
    w_attr = centred(splits[10], (HID, F_IN), HID ** -0.5, 0.375)
    attr_bias = centred(splits[11], (F_IN,), 0.5, 3.0, (), jnp.float32)
    return {"attributes": attributes, "adj_values": adj_values, "adj_rows": adj_rows, "adj_cols": adj_cols, "adj_count": adj_count, "pair_ids": pair_ids, "struct_target": struct_target, "w_first": w_first, "w_rest": w_rest, "layer_bias": layer_bias, "w_attr": w_attr, "attr_bias": attr_bias}


epsilon = 1e-06
mix_alpha = 0.8

def tile_partial(panel_blocks, block_vals, row_ids, col_ids, live_mask):
    group_size = math.gcd(K_CAP, 32)
    num_groups = K_CAP // group_size

    def add_group(partial_sum, group_index):
        start = group_index * group_size
        vals_now = lax.dynamic_slice_in_dim(block_vals, start, group_size, 0).astype(jnp.float32)
        rows_now = lax.dynamic_slice_in_dim(row_ids, start, group_size, 0)
        cols_now = lax.dynamic_slice_in_dim(col_ids, start, group_size, 0)
        mask_now = lax.dynamic_slice_in_dim(live_mask, start, group_size, 0)
        picked = jnp.take(panel_blocks, cols_now, axis=0).astype(jnp.float32)
        products = jnp.einsum('gij,gjf->gif', vals_now, picked)
        return (partial_sum.at[rows_now].add(products * mask_now[:, None, None]), None)
    initial = jnp.zeros((TILE_ROWB, BLK, HID), jnp.float32)
    result, _ = lax.scan(add_group, initial, jnp.arange(num_groups, dtype=jnp.int32))
    return result

def aggregate(features, adj_values, adj_rows, adj_cols, live_all):
    grouped = features.reshape(N_ROW, N_COL, V_DEV, HID)

    def add_tile(total_sum, tile_index):
        row_index = tile_index // N_COL
        col_index = tile_index % N_COL
        column_group = lax.dynamic_index_in_dim(grouped, col_index, 1, False).reshape(TILE_COLB, BLK, HID)
        block_vals = lax.dynamic_index_in_dim(lax.dynamic_index_in_dim(adj_values, row_index, 0, False), col_index, 0, False)
        row_ids = lax.dynamic_index_in_dim(lax.dynamic_index_in_dim(adj_rows, row_index, 0, False), col_index, 0, False)
        col_ids = lax.dynamic_index_in_dim(lax.dynamic_index_in_dim(adj_cols, row_index, 0, False), col_index, 0, False)
        live_mask = lax.dynamic_index_in_dim(lax.dynamic_index_in_dim(live_all, row_index, 0, False), col_index, 0, False)
        partial_sum = tile_partial(column_group, block_vals, row_ids, col_ids, live_mask)
        current = lax.dynamic_index_in_dim(total_sum, row_index, 0, False)
        return (lax.dynamic_update_index_in_dim(total_sum, current + partial_sum, row_index, 0), None)
    initial = jnp.zeros((N_ROW, TILE_ROWB, BLK, HID), jnp.float32)
    total_sum, _ = lax.scan(add_tile, initial, jnp.arange(N_ROW * N_COL, dtype=jnp.int32))
    return total_sum.reshape(NODES, HID)

def reference(attributes, adj_values, adj_rows, adj_cols, adj_count, pair_ids, struct_target, w_first, w_rest, layer_bias, w_attr, attr_bias):
    slot_ids = jnp.arange(K_CAP, dtype=jnp.int32)
    live_all = (slot_ids[None, None, :] < adj_count[:, :, None]).astype(jnp.float32)
    row_mass = lax.optimization_barrier(jnp.sum(adj_values, axis=-1, dtype=jnp.float32)) * live_all[..., None]
    group_ids = jnp.broadcast_to(jnp.arange(N_ROW, dtype=jnp.int32)[:, None, None], adj_rows.shape)
    degree_terms = jnp.zeros((N_ROW, TILE_ROWB, BLK), jnp.float32).at[group_ids, adj_rows].add(row_mass)
    row_scale = lax.rsqrt(1.0 + degree_terms.reshape(NODES))
    hidden_state = attributes
    for layer_index in range(LAYERS):
        weight = w_first if layer_index == 0 else w_rest[layer_index - 1]
        projected = jnp.dot(hidden_state, weight, preferred_element_type=jnp.float32)
        features = projected[:, :HID].astype(jnp.bfloat16)
        summed = aggregate(features, adj_values, adj_rows, adj_cols, live_all)
        before = row_scale[:, None] * summed + projected[:, HID:]
        if layer_index > 0:
            before = before + layer_bias[layer_index - 1]
        hidden_state = jnp.tanh(before).astype(jnp.bfloat16)
    embedding = hidden_state
    rebuilt = jnp.dot(embedding, w_attr, preferred_element_type=jnp.float32) + attr_bias
    attr_error = jnp.sqrt(lax.optimization_barrier(jnp.mean((rebuilt - attributes.astype(jnp.float32)) ** 2, axis=1)) + epsilon)
    span_blocks = embedding.reshape(N_ROW * N_COL, BLOCKS_DEV, BLK, HID)
    all_blocks = embedding.reshape(NODE_BLOCKS, BLK, HID)
    span_pairs = pair_ids.reshape(N_ROW * N_COL, BLOCKS_DEV, PAIRS)
    span_target = struct_target.reshape(N_ROW * N_COL, V_DEV, PAIRS, BLK)

    def span_error(span_index):
        col_index = span_index % N_COL
        own_blocks = lax.dynamic_index_in_dim(span_blocks, span_index, 0, False).astype(jnp.float32)
        partner_ids = lax.dynamic_index_in_dim(span_pairs, span_index, 0, False)
        global_ids = (partner_ids // BLOCKS_DEV * N_COL + col_index) * BLOCKS_DEV + partner_ids % BLOCKS_DEV
        partners = jnp.take(all_blocks, global_ids.astype(jnp.int32), axis=0).astype(jnp.float32)
        logits = jnp.einsum('bif,bpjf->bipj', own_blocks, partners) * HID ** (-0.5)
        probability = jax.nn.sigmoid(logits).reshape(V_DEV, PAIRS, BLK)
        target = lax.dynamic_index_in_dim(span_target, span_index, 0, False).astype(jnp.float32)
        return jnp.sqrt(lax.optimization_barrier(jnp.mean((probability - target) ** 2, axis=(1, 2))) + epsilon)
    struct_error = lax.map(span_error, jnp.arange(N_ROW * N_COL, dtype=jnp.int32)).reshape(NODES)
    return mix_alpha * attr_error + (1.0 - mix_alpha) * struct_error
```

```python
import functools

import jax
import jax.numpy as jnp
from jax import lax
from jax.experimental import pallas as pl
from jax.experimental.pallas import tpu as pltpu
from jax.sharding import PartitionSpec as P

epsilon = 1e-06
mix_alpha = 0.8

BLK = 128
N_X, N_Y = 4, 4
N_ROW, N_COL = 8, 16
DEV_BLOCKS = 4
HALF_BLOCKS = 32
RING = 64
UNROLL = 4


def row_of(x, z_lo):
    return (x % N_X) * 2 + z_lo


def col_of(y, z_hi, core):
    return ((y % N_Y) * 2 + z_hi) * 2 + core


def shift_row(value, dx, dz):
    perm = [(row_of(x, z), row_of(x + dx, z ^ dz)) for x in range(N_X) for z in range(2)]
    return lax.ppermute(value, "row", perm)


def shift_col(value, dy, dz, dc):
    perm = [
        (col_of(y, z, c), col_of(y + dy, z ^ dz, c ^ dc))
        for y in range(N_Y)
        for z in range(2)
        for c in range(2)
    ]
    return lax.ppermute(value, "col", perm)


def gather_row(own):
    half = own.shape[0] // 2
    from_z = shift_row(own, 0, 1)
    from_left = shift_row(own, 1, 0)
    from_right = shift_row(own, -1, 0)
    far = shift_row(from_right, -1, 0)
    left_z = shift_row(from_z, 1, 0)
    right_z = shift_row(from_right, 0, 1)
    far_z_top = shift_row(left_z[:half], 1, 0)
    far_z_bottom = shift_row(right_z[half:], -1, 0)
    return [own, from_z, from_right, right_z, far, (far_z_top, far_z_bottom), from_left, left_z]


def add(*values):
    total = values[0].astype(jnp.float32)
    for value in values[1:]:
        total = total + value.astype(jnp.float32)
    return total


def scatter_col(send, keep):
    got = shift_col(send, 0, 0, 1)

    def pair(dy, dz, *more):
        at = dy * 2 + dz
        return add(keep[at], got[at], *more)

    low = jnp.bfloat16
    far_up = shift_col(pair(2, 0).astype(low), 1, 0, 0)
    far_down = shift_col(pair(2, 1).astype(low), -1, 0, 0)
    direct_up = shift_col(pair(1, 1).astype(low), 1, 0, 0)
    direct_down = shift_col(pair(3, 0).astype(low), -1, 0, 0)
    relay_up = shift_col(pair(1, 0, far_up).astype(low), 1, 0, 0)
    relay_down = shift_col(pair(3, 1, far_down).astype(low), -1, 0, 0)
    other = pair(0, 1, relay_down, direct_up).astype(low)
    from_other = shift_col(other, 0, 1, 0)
    return pair(0, 0, relay_up, direct_down, from_other)


def spmm_kernel(with_degree, half, count_ref, first_ref, second_ref, *refs):
    pieces = refs[:9]
    vals_ref = refs[9]
    out_ref = refs[10]
    panel, total, ring, ring_sem, panel_sem = refs[11:16]
    width = pieces[0].shape[-1]
    rows_half = pieces[5].shape[0]

    groups = (count_ref[half] + UNROLL - 1) // UNROLL
    pairs = groups * UNROLL

    def copies(pair, slot):
        a = first_ref[half, pair] & 511
        b = second_ref[half, pair] & 511
        return (
            pltpu.make_async_copy(vals_ref.at[a], ring.at[slot, 0], ring_sem.at[slot, 0]),
            pltpu.make_async_copy(vals_ref.at[b], ring.at[slot, 1], ring_sem.at[slot, 1]),
        )

    def start(pair, slot):
        for copy in copies(pair, slot):
            copy.start()

    panel_copies = []
    at = 0
    for index, piece in enumerate(pieces):
        blocks = piece.shape[0]
        panel_copies.append(
            pltpu.make_async_copy(
                piece,
                panel.at[pl.ds(at, blocks), :, pl.ds(0, width)],
                panel_sem.at[index],
            )
        )
        at += blocks
    for copy in panel_copies:
        copy.start()

    @pl.loop(0, jnp.minimum(pairs, RING))
    def _(pair):
        start(pair, pair)

    panel[N_ROW * DEV_BLOCKS] = jnp.zeros(panel.shape[1:], panel.dtype)
    if with_degree:

        @pl.loop(0, N_ROW * DEV_BLOCKS)
        def _(block):
            panel[block, :, width:] = jnp.ones((BLK, panel.shape[2] - width), panel.dtype)

    @pl.loop(0, HALF_BLOCKS)
    def _(block):
        total[block] = jnp.zeros(total.shape[1:], jnp.float32)

    for copy in panel_copies:
        copy.wait()

    @pl.loop(0, groups)
    def _(group):
        base = (group % (RING // UNROLL)) * UNROLL
        for u in range(UNROLL):
            pair = group * UNROLL + u
            slot = base + u
            for copy in copies(pair, slot):
                copy.wait()
        for u in range(UNROLL):
            pair = group * UNROLL + u
            slot = base + u
            first = first_ref[half, pair]
            second = second_ref[half, pair]
            row = lax.shift_right_logical(first, 15)
            col_a = lax.shift_right_logical(first, 9) & 63
            col_b = lax.shift_right_logical(second, 9) & 63
            left = jnp.concatenate([ring[slot, 0], ring[slot, 1]], axis=1)
            right = jnp.concatenate([panel[col_a], panel[col_b]], axis=0)
            total[row] += jnp.dot(left, right, preferred_element_type=jnp.float32)
        for u in range(UNROLL):
            pair = group * UNROLL + u
            slot = base + u

            @pl.when(pair + RING < pairs)
            def _():
                start(pair + RING, slot)

    if with_degree:
        degree = refs[16]
        degree[...] = jnp.zeros(degree.shape, jnp.float32)
        eye = lax.broadcasted_iota(jnp.int32, (BLK, BLK), 0) == lax.broadcasted_iota(
            jnp.int32, (BLK, BLK), 1
        )

    @pl.loop(0, HALF_BLOCKS // DEV_BLOCKS)
    def _(dest):
        for j in range(DEV_BLOCKS):
            block = dest * DEV_BLOCKS + j
            out_ref[dest, pl.ds(j * BLK, BLK), :] = total[block, :, :width].astype(out_ref.dtype)
            if with_degree:
                spread = jnp.where(eye, total[block, :, width:], 0.0)
                degree[j : j + 1, :] = jnp.sum(spread, axis=0, keepdims=True)
        if with_degree:
            out_ref[dest, pl.ds(DEV_BLOCKS * BLK, 16), :] = degree[...].astype(out_ref.dtype)


def spmm(pieces, vals, plan, half, with_degree):
    count, first, second = plan
    flat = []
    for piece in pieces:
        for part in piece if isinstance(piece, tuple) else (piece,):
            flat.append(part.reshape(-1, BLK, part.shape[-1]))
    width = flat[0].shape[-1]
    rows = DEV_BLOCKS * BLK + (16 if with_degree else 0)
    wide = width + (BLK if with_degree else 0)
    scratch = [
        pltpu.VMEM((N_ROW * DEV_BLOCKS + 1, BLK, wide), jnp.bfloat16),
        pltpu.VMEM((HALF_BLOCKS, BLK, wide), jnp.float32),
        pltpu.VMEM((RING, 2, BLK, BLK), jnp.bfloat16),
        pltpu.SemaphoreType.DMA((RING, 2)),
        pltpu.SemaphoreType.DMA((len(flat),)),
    ]
    if with_degree:
        scratch.append(pltpu.VMEM((16, BLK), jnp.float32))
    any_spec = pl.BlockSpec(memory_space=pl.ANY)
    smem = pl.BlockSpec(memory_space=pltpu.SMEM)
    return pl.pallas_call(
        functools.partial(spmm_kernel, with_degree, half),
        out_shape=jax.ShapeDtypeStruct((HALF_BLOCKS // DEV_BLOCKS, rows, width), jnp.bfloat16),
        in_specs=[smem] * 3 + [any_spec] * (len(flat) + 1),
        out_specs=pl.BlockSpec(memory_space=pltpu.VMEM),
        scratch_shapes=scratch,
        compiler_params=pltpu.CompilerParams(vmem_limit_bytes=24 * 1024 * 1024),
        cost_estimate=pl.CostEstimate(
            flops=2 * 208 * BLK * 256 * 256, bytes_accessed=8 * 1024 * 1024, transcendentals=0
        ),
        name="spmm_keep" if half else "spmm_send",
    )(count, first, second, *flat, vals)


def make_plan(row_ids, col_ids, live_count, row_at, col_at):
    capacity = row_ids.shape[0]
    slots = jnp.arange(capacity, dtype=jnp.int32)
    live = slots < live_count
    x, z_lo = row_at // 2, row_at % 2
    y, z_hi, core = col_at // 4, (col_at // 2) % 2, col_at % 2
    dest, j = row_ids // DEV_BLOCKS, row_ids % DEV_BLOCKS
    dy = (dest // 4 - y) % N_Y
    dz = (dest // 2 + z_hi) % 2
    dc = (dest + core) % 2
    row = (1 - dc) * HALF_BLOCKS + (dy * 2 + dz) * DEV_BLOCKS + j
    col = relative_block(col_ids, x, z_lo)
    row_key = jnp.where(live, row, 2 * HALF_BLOCKS)
    same = (row_key[:, None] == row_key[None, :]) & live[None, :]
    within = jnp.sum((same & (slots[None, :] < slots[:, None])).astype(jnp.int32), axis=1)
    opens = live & (within % 2 == 0)
    same_half = (row_key[:, None] // HALF_BLOCKS) == (row_key[None, :] // HALF_BLOCKS)
    ahead = (row_key[None, :] < row_key[:, None]) & same_half & opens[None, :]
    pair = jnp.sum(ahead.astype(jnp.int32), axis=1) + within // 2
    half = row_key // HALF_BLOCKS
    longest = (capacity + HALF_BLOCKS) // 2 + UNROLL
    places = jnp.arange(longest, dtype=jnp.int32)
    word = slots + col * 512 + (row % HALF_BLOCKS) * (512 * 64) - N_ROW * DEV_BLOCKS * 512

    def lay(side):
        out = []
        for h in range(2):
            here = (within % 2 == side) & (half == h)
            hit = (pair[None, :] == places[:, None]) & here[None, :]
            out.append(
                N_ROW * DEV_BLOCKS * 512 + jnp.sum(jnp.where(hit, word[None, :], 0), axis=1)
            )
        return jnp.stack(out).astype(jnp.int32)

    count = jnp.stack(
        [jnp.sum((opens & (half == h)).astype(jnp.int32)) for h in range(2)]
    ).astype(jnp.int32)
    return count, lay(0), lay(1)


def relative_block(ids, x, z_lo):
    owner, j = ids // DEV_BLOCKS, ids % DEV_BLOCKS
    return (((owner // 2 - x) % N_X) * 2 + (owner + z_lo) % 2) * DEV_BLOCKS + j


def per_device(
    attributes,
    adj_values,
    adj_rows,
    adj_cols,
    adj_count,
    pair_ids,
    struct_target,
    w_first,
    w_rest,
    layer_bias,
    w_attr,
    attr_bias,
):
    vals = adj_values[0, 0]
    nodes_dev = attributes.shape[0]
    hidden_size = w_rest.shape[1]
    pair_count = pair_ids.shape[1]
    row_at = lax.axis_index("row")
    col_at = lax.axis_index("col")
    plan = make_plan(adj_rows[0, 0], adj_cols[0, 0], adj_count[0, 0], row_at, col_at)

    pieces = gather_row(attributes)
    send = spmm(pieces, vals, plan, 0, True)
    keep = spmm(pieces, vals, plan, 1, True)
    summed = scatter_col(send, keep)
    degree = 1.0 + summed[nodes_dev : nodes_dev + DEV_BLOCKS].reshape(-1)
    row_scale = lax.rsqrt(degree)[:, None]
    aggregate = summed[:nodes_dev]
    coarse = lax.reduce_precision(aggregate, 8, 7)
    fine = (aggregate - coarse).astype(jnp.bfloat16)
    coarse = coarse.astype(jnp.bfloat16)
    w_near, w_self = w_first[:, :hidden_size], w_first[:, hidden_size:]
    own_part = jnp.dot(attributes, w_self, preferred_element_type=jnp.float32)
    mixed = jnp.dot(coarse, w_near, preferred_element_type=jnp.float32) + jnp.dot(
        fine, w_near, preferred_element_type=jnp.float32
    )
    hidden_state = jnp.tanh(row_scale * mixed + own_part).astype(jnp.bfloat16)

    features = jnp.dot(
        hidden_state, w_rest[0][:, :hidden_size], preferred_element_type=jnp.float32
    ).astype(jnp.bfloat16)
    pieces = gather_row(features)
    own_part = (
        jnp.dot(hidden_state, w_rest[0][:, hidden_size:], preferred_element_type=jnp.float32)
        + layer_bias[0]
    )
    send = spmm(pieces, vals, plan, 0, False)
    keep = spmm(pieces, vals, plan, 1, False)
    summed = scatter_col(send, keep)
    hidden_state = jnp.tanh(row_scale * summed + own_part).astype(jnp.bfloat16)

    pieces = gather_row(hidden_state)
    rebuilt = jnp.dot(hidden_state, w_attr, preferred_element_type=jnp.float32) + attr_bias
    attr_error = jnp.sqrt(
        jnp.mean((rebuilt - attributes.astype(jnp.float32)) ** 2, axis=1) + epsilon
    )
    whole = jnp.concatenate(
        [part for piece in pieces for part in (piece if isinstance(piece, tuple) else (piece,))]
    ).reshape(-1, BLK, hidden_size)
    own_blocks = hidden_state.reshape(-1, BLK, hidden_size)
    partners = jnp.take(whole, relative_block(pair_ids, row_at // 2, row_at % 2), axis=0)
    logits = jnp.einsum(
        "bif,bpjf->bipj", own_blocks, partners, preferred_element_type=jnp.float32
    ) * hidden_size ** (-0.5)
    probability = jax.nn.sigmoid(logits).reshape(nodes_dev, pair_count, BLK)
    struct_error = jnp.sqrt(
        jnp.mean((probability - struct_target.astype(jnp.float32)) ** 2, axis=(1, 2)) + epsilon
    )
    return mix_alpha * attr_error + (1.0 - mix_alpha) * struct_error


def solution(mesh):
    return jax.shard_map(
        per_device,
        mesh=mesh,
        in_specs=(
            P(("row", "col"), None),
            P("row", "col", None, None, None),
            P("row", "col", None),
            P("row", "col", None),
            P("row", "col"),
            P(("row", "col"), None),
            P(("row", "col"), None, None),
            P(),
            P(),
            P(),
            P(),
            P(),
        ),
        out_specs=P(("row", "col")),
        check_vma=False,
    )
```

```python
import functools

import jax
import jax.numpy as jnp
from jax import lax
from jax.experimental import pallas as pl
from jax.experimental.pallas import tpu as pltpu
from jax.sharding import PartitionSpec as P

epsilon = 1e-06
mix_alpha = 0.8

BLK = 128
N_X, N_Y = 4, 4
N_ROW, N_COL = 8, 16
DEV_BLOCKS = 4
PANEL_BLOCKS = N_ROW * DEV_BLOCKS
DEST = 8
CHUNKS = 1
CHUNK_BLOCKS = DEV_BLOCKS // CHUNKS
PART_BLOCKS = DEST * CHUNK_BLOCKS
UNROLL = 8


def row_of(x, z_lo):
    return (x % N_X) * 2 + z_lo


def col_of(y, z_hi, core):
    return ((y % N_Y) * 2 + z_hi) * 2 + core


def shift_row(value, dx, dz):
    perm = [(row_of(x, z), row_of(x + dx, z ^ dz)) for x in range(N_X) for z in range(2)]
    return lax.ppermute(value, "row", perm)


def shift_col(value, dy, dz, dc):
    perm = [
        (col_of(y, z, c), col_of(y + dy, z ^ dz, c ^ dc))
        for y in range(N_Y)
        for z in range(2)
        for c in range(2)
    ]
    return lax.ppermute(value, "col", perm)


def gather_row(own, first_block=0):
    half = own.shape[0] // 2
    from_z = shift_row(own, 0, 1)
    from_left = shift_row(own, 1, 0)
    from_right = shift_row(own, -1, 0)
    far = shift_row(from_right, -1, 0)
    left_z = shift_row(from_z, 1, 0)
    right_z = shift_row(from_right, 0, 1)
    far_z_top = shift_row(left_z[:half], 1, 0)
    far_z_bottom = shift_row(right_z[half:], -1, 0)
    placed = [
        (0, own),
        (1, from_z),
        (2, from_right),
        (3, right_z),
        (4, far),
        (5, far_z_top),
        (6, from_left),
        (7, left_z),
    ]
    out = [(at * DEV_BLOCKS + first_block, piece) for at, piece in placed]
    out.append((5 * DEV_BLOCKS + first_block + half // BLK, far_z_bottom))
    return out


def add(*values):
    total = values[0].astype(jnp.float32)
    for value in values[1:]:
        total = total + value.astype(jnp.float32)
    return total


def scatter_col(send, keep):
    got = shift_col(send, 0, 0, 1)

    def pair(dy, dz, *more):
        at = dy * 2 + dz
        return add(keep[at], got[at], *more)

    low = jnp.bfloat16
    far_up = shift_col(pair(2, 0).astype(low), 1, 0, 0)
    far_down = shift_col(pair(2, 1).astype(low), -1, 0, 0)
    direct_up = shift_col(pair(1, 1).astype(low), 1, 0, 0)
    direct_down = shift_col(pair(3, 0).astype(low), -1, 0, 0)
    relay_up = shift_col(pair(1, 0, far_up).astype(low), 1, 0, 0)
    relay_down = shift_col(pair(3, 1, far_down).astype(low), -1, 0, 0)
    other = pair(0, 1, relay_down, direct_up).astype(low)
    from_other = shift_col(other, 0, 1, 0)
    return pair(0, 0, relay_up, direct_down, from_other)


def params(mib):
    return pltpu.CompilerParams(vmem_limit_bytes=mib * 1024 * 1024)


any_spec = pl.BlockSpec(memory_space=pl.ANY)
smem_spec = pl.BlockSpec(memory_space=pltpu.SMEM)
vmem_spec = pl.BlockSpec(memory_space=pltpu.VMEM)


def preload_kernel(source, target, sem):
    copy = pltpu.make_async_copy(source, target, sem)
    copy.start()
    copy.wait()


def preload(vals):
    return pl.pallas_call(
        preload_kernel,
        out_shape=pltpu.VMEM(vals.shape, vals.dtype),
        in_specs=[pl.BlockSpec(memory_space=pltpu.HBM)],
        out_specs=vmem_spec,
        scratch_shapes=[pltpu.SemaphoreType.DMA(())],
        compiler_params=params(16),
        cost_estimate=pl.CostEstimate(flops=0, bytes_accessed=2 * vals.size, transcendentals=0),
        name="load_blocks",
    )(vals)


def start_panel(pieces, starts, panel, sems):
    copies = []
    for index, (piece, start) in enumerate(zip(pieces, starts)):
        where = panel.at[pl.ds(start, piece.shape[0]), :, pl.ds(0, piece.shape[2])]
        copies.append(pltpu.make_async_copy(piece, where, sems.at[index]))
    for copy in copies:
        copy.start()
    return copies


def panel_kernel(starts, fill, *refs):
    pieces = refs[: len(starts)]
    panel, sems = refs[len(starts) :]
    copies = start_panel(pieces, starts, panel, sems)
    panel[PANEL_BLOCKS] = jnp.zeros(panel.shape[1:], panel.dtype)
    width = pieces[0].shape[2]
    if fill:

        @pl.loop(0, PANEL_BLOCKS)
        def _(block):
            panel[block, :, width:] = jnp.ones((BLK, panel.shape[2] - width), panel.dtype)

    for copy in copies:
        copy.wait()


def make_panel(placed, fill):
    starts = [start for start, _ in placed]
    pieces = [piece.reshape(-1, BLK, piece.shape[-1]) for _, piece in placed]
    width = pieces[0].shape[-1] + (BLK if fill else 0)
    return pl.pallas_call(
        functools.partial(panel_kernel, starts, fill),
        out_shape=pltpu.VMEM((PANEL_BLOCKS + 1, BLK, width), jnp.bfloat16),
        in_specs=[any_spec] * len(pieces),
        out_specs=vmem_spec,
        scratch_shapes=[pltpu.SemaphoreType.DMA((len(pieces),))],
        compiler_params=params(16),
        name="panel",
    )(*pieces)


def spmm_kernel(with_degree, part, count_ref, first_ref, second_ref, panel, vals, out_ref, *refs):
    total = refs[0]
    width = out_ref.shape[-1]

    @pl.loop(0, PART_BLOCKS)
    def _(block):
        total[block] = jnp.zeros(total.shape[1:], jnp.float32)

    @pl.loop(0, (count_ref[part] + UNROLL - 1) // UNROLL)
    def _(group):
        for u in range(UNROLL):
            first = first_ref[part, group * UNROLL + u]
            second = second_ref[part, group * UNROLL + u]
            row = lax.shift_right_logical(first, 15)
            col_a = lax.shift_right_logical(first, 9) & 63
            col_b = lax.shift_right_logical(second, 9) & 63
            left = jnp.concatenate([vals[first & 511], vals[second & 511]], axis=1)
            right = jnp.concatenate([panel[col_a], panel[col_b]], axis=0)
            total[row] += jnp.dot(left, right, preferred_element_type=jnp.float32)

    if with_degree:
        degree = refs[1]
        degree[...] = jnp.zeros(degree.shape, jnp.float32)
        eye = lax.broadcasted_iota(jnp.int32, (BLK, BLK), 0) == lax.broadcasted_iota(
            jnp.int32, (BLK, BLK), 1
        )

    @pl.loop(0, DEST)
    def _(dest):
        for j in range(CHUNK_BLOCKS):
            block = dest * CHUNK_BLOCKS + j
            out_ref[dest, pl.ds(j * BLK, BLK), :] = total[block, :, :width].astype(out_ref.dtype)
            if with_degree:
                spread = jnp.where(eye, total[block, :, width:], 0.0)
                degree[j : j + 1, :] = jnp.sum(spread, axis=0, keepdims=True)
        if with_degree:
            out_ref[dest, pl.ds(CHUNK_BLOCKS * BLK, 16), :] = degree[...].astype(out_ref.dtype)


def spmm(panel, vals, plan, part, with_degree):
    wide = panel.shape[2]
    width = wide - BLK if with_degree else wide
    rows = CHUNK_BLOCKS * BLK + (16 if with_degree else 0)
    scratch = [pltpu.VMEM((PART_BLOCKS, BLK, wide), jnp.float32)]
    if with_degree:
        scratch.append(pltpu.VMEM((16, BLK), jnp.float32))
    return pl.pallas_call(
        functools.partial(spmm_kernel, with_degree, part),
        out_shape=jax.ShapeDtypeStruct((DEST, rows, width), jnp.bfloat16),
        in_specs=[smem_spec] * 3 + [vmem_spec] * 2,
        out_specs=vmem_spec,
        scratch_shapes=scratch,
        compiler_params=params(16),
        cost_estimate=pl.CostEstimate(
            flops=2 * 208 * BLK * 256 * 256 // CHUNKS,
            bytes_accessed=4 * 1024 * 1024 // CHUNKS,
            transcendentals=0,
        ),
        name="product_keep" if part % 2 else "product_send",
    )(*plan, panel, vals)


def score_kernel(starts, pair_ref, own, target, attributes, w_attr, attr_bias, *refs):
    pieces = refs[: len(starts)]
    out_ref, panel, sems = refs[len(starts) :]
    copies = start_panel(pieces, starts, panel, sems)
    scale = own.shape[1] ** (-0.5)
    n_pair = pair_ref.shape[1]

    def row_mean(squares, count):
        return jnp.sum(squares.T, axis=0, keepdims=True) / count

    errors = []
    for block in range(DEV_BLOCKS):
        rows = pl.ds(block * BLK, BLK)
        rebuilt = jnp.dot(own[rows, :], w_attr[...], preferred_element_type=jnp.float32)
        gap = rebuilt + attr_bias[...] - attributes[rows, :].astype(jnp.float32)
        errors.append(jnp.sqrt(row_mean(gap * gap, gap.shape[1]) + epsilon))
    for copy in copies:
        copy.wait()
    for block in range(DEV_BLOCKS):
        rows = pl.ds(block * BLK, BLK)
        squares = jnp.zeros((BLK, BLK), jnp.float32)
        for pair in range(n_pair):
            logits = lax.dot_general(
                own[rows, :],
                panel[pair_ref[block, pair]],
                (((1,), (1,)), ((), ())),
                preferred_element_type=jnp.float32,
            )
            gap = jax.nn.sigmoid(logits * scale) - target[rows, pl.ds(pair * BLK, BLK)].astype(
                jnp.float32
            )
            squares = squares + gap * gap
        struct = jnp.sqrt(row_mean(squares, n_pair * BLK) + epsilon)
        out_ref[block : block + 1, :] = mix_alpha * errors[block] + (1.0 - mix_alpha) * struct


def score(placed, pairs, own, target, attributes, w_attr, attr_bias):
    starts = [start for start, _ in placed]
    pieces = [piece.reshape(-1, BLK, piece.shape[-1]) for _, piece in placed]
    out = pl.pallas_call(
        functools.partial(score_kernel, starts),
        out_shape=jax.ShapeDtypeStruct((DEV_BLOCKS, BLK), jnp.float32),
        in_specs=[smem_spec] + [vmem_spec] * 5 + [any_spec] * len(pieces),
        out_specs=vmem_spec,
        scratch_shapes=[
            pltpu.VMEM((PANEL_BLOCKS, BLK, own.shape[1]), jnp.bfloat16),
            pltpu.SemaphoreType.DMA((len(pieces),)),
        ],
        compiler_params=params(16),
        name="score",
    )(pairs, own, target, attributes, w_attr, attr_bias, *pieces)
    return out.reshape(-1)


def make_plan(row_ids, col_ids, live_count, row_at, col_at):
    capacity = row_ids.shape[0]
    parts = 2 * CHUNKS
    slots = jnp.arange(capacity, dtype=jnp.int32)
    live = slots < live_count
    y, z_hi, core = col_at // 4, (col_at // 2) % 2, col_at % 2
    dest, j = row_ids // DEV_BLOCKS, row_ids % DEV_BLOCKS
    dy = (dest // 4 - y) % N_Y
    dz = (dest // 2 + z_hi) % 2
    dc = (dest + core) % 2
    part = (j // CHUNK_BLOCKS) * 2 + 1 - dc
    row = (dy * 2 + dz) * CHUNK_BLOCKS + j % CHUNK_BLOCKS
    key = part * PART_BLOCKS + row
    col = relative_block(col_ids, row_at)
    same = (key[:, None] == key[None, :]) & live[None, :]
    within = jnp.sum((same & (slots[None, :] < slots[:, None])).astype(jnp.int32), axis=1)
    opens = live & (within % 2 == 0)
    ahead = (key[None, :] < key[:, None]) & (part[None, :] == part[:, None]) & opens[None, :]
    pair = jnp.sum(ahead.astype(jnp.int32), axis=1) + within // 2
    longest = -(-((capacity + PART_BLOCKS) // 2) // UNROLL) * UNROLL
    place = jnp.where(live, (part * longest + pair) * 2 + within % 2, -1)
    places = jnp.arange(parts * longest, dtype=jnp.int32)
    empty = PANEL_BLOCKS * 512
    word = slots + col * 512 + row * (512 * 64) - empty

    def lay(side):
        hit = place[None, :] == (places * 2 + side)[:, None]
        return (empty + jnp.sum(jnp.where(hit, word[None, :], 0), axis=1)).reshape(parts, longest)

    count = jnp.sum(
        (opens[None, :] & (part[None, :] == jnp.arange(parts)[:, None])).astype(jnp.int32), axis=1
    )
    return count, lay(0), lay(1)


def relative_block(ids, row_at):
    owner, j = ids // DEV_BLOCKS, ids % DEV_BLOCKS
    dx = (owner // 2 - row_at // 2) % N_X
    return (dx * 2 + (owner + row_at) % 2) * DEV_BLOCKS + j


def per_device(
    attributes,
    adj_values,
    adj_rows,
    adj_cols,
    adj_count,
    pair_ids,
    struct_target,
    w_first,
    w_rest,
    layer_bias,
    w_attr,
    attr_bias,
):
    vals = preload(adj_values[0, 0])
    hidden_size = w_rest.shape[1]
    row_at = lax.axis_index("row")
    col_at = lax.axis_index("col")
    plan = make_plan(adj_rows[0, 0], adj_cols[0, 0], adj_count[0, 0], row_at, col_at)
    chunk = CHUNK_BLOCKS * BLK
    w_near, w_self = w_first[:, :hidden_size], w_first[:, hidden_size:]
    own_part = jnp.dot(attributes, w_self, preferred_element_type=jnp.float32)

    panel = make_panel(gather_row(attributes), True)
    placed, scales, own_second = [], [], []
    products = [spmm(panel, vals, plan, part, True) for part in range(2 * CHUNKS)]
    for c in range(CHUNKS):
        summed = scatter_col(products[2 * c], products[2 * c + 1])
        degree = 1.0 + summed[chunk : chunk + CHUNK_BLOCKS].reshape(-1)
        row_scale = lax.rsqrt(degree)[:, None]
        aggregate = summed[:chunk]
        coarse = lax.reduce_precision(aggregate, 8, 7)
        fine = (aggregate - coarse).astype(jnp.bfloat16)
        coarse = coarse.astype(jnp.bfloat16)
        mixed = jnp.dot(coarse, w_near, preferred_element_type=jnp.float32) + jnp.dot(
            fine, w_near, preferred_element_type=jnp.float32
        )
        before = row_scale * mixed + own_part[c * chunk : (c + 1) * chunk]
        hidden = jnp.tanh(before).astype(jnp.bfloat16)
        features = jnp.dot(
            hidden, w_rest[0][:, :hidden_size], preferred_element_type=jnp.float32
        ).astype(jnp.bfloat16)
        placed += gather_row(features, c * CHUNK_BLOCKS)
        scales.append(row_scale)
        own_second.append(
            jnp.dot(hidden, w_rest[0][:, hidden_size:], preferred_element_type=jnp.float32)
            + layer_bias[0]
        )

    panel = make_panel(placed, False)
    placed, embedding = [], []
    products = [spmm(panel, vals, plan, part, False) for part in range(2 * CHUNKS)]
    for c in range(CHUNKS):
        summed = scatter_col(products[2 * c], products[2 * c + 1])
        hidden = jnp.tanh(scales[c] * summed + own_second[c]).astype(jnp.bfloat16)
        embedding.append(hidden)
        placed += gather_row(hidden, c * CHUNK_BLOCKS)

    return score(
        placed,
        relative_block(pair_ids, row_at),
        jnp.concatenate(embedding),
        struct_target.reshape(struct_target.shape[0], -1),
        attributes,
        w_attr,
        attr_bias[None, :],
    )


def solution(mesh):
    return jax.shard_map(
        per_device,
        mesh=mesh,
        in_specs=(
            P(("row", "col"), None),
            P("row", "col", None, None, None),
            P("row", "col", None),
            P("row", "col", None),
            P("row", "col"),
            P(("row", "col"), None),
            P(("row", "col"), None, None),
            P(),
            P(),
            P(),
            P(),
            P(),
        ),
        out_specs=P(("row", "col")),
        check_vma=False,
    )
```

```python
import functools

import jax
import jax.numpy as jnp
from jax import lax
from jax.experimental import pallas as pl
from jax.experimental.pallas import tpu as pltpu
from jax.sharding import PartitionSpec as P

epsilon = 1e-06
mix_alpha = 0.8

BLK = 128
N_X, N_Y = 4, 4
N_ROW, N_COL = 8, 16
DEV_BLOCKS = 4
DEST = 8
HALF_BLOCKS = DEST * DEV_BLOCKS
HOP = (0, 0, 0, 1, 1, 1, 0, 1)
PLACE = (0, 1, 2, 0, 1, 3, 3, 2)
UNROLL = 8


def row_of(x, z_lo):
    return (x % N_X) * 2 + z_lo


def col_of(y, z_hi, core):
    return ((y % N_Y) * 2 + z_hi) * 2 + core


def shift_row(value, dx, dz):
    perm = [(row_of(x, z), row_of(x + dx, z ^ dz)) for x in range(N_X) for z in range(2)]
    return lax.ppermute(value, "row", perm)


def shift_col(value, dy, dz, dc):
    perm = [
        (col_of(y, z, c), col_of(y + dy, z ^ dz, c ^ dc))
        for y in range(N_Y)
        for z in range(2)
        for c in range(2)
    ]
    return lax.ppermute(value, "col", perm)


def gather_row(own):
    half = own.shape[0] // 2
    from_left = shift_row(own, 1, 0)
    from_right = shift_row(own, -1, 0)
    from_z = shift_row(own, 0, 1)
    far = shift_row(from_right, -1, 0)
    left_z = shift_row(from_z, 1, 0)
    right_z = shift_row(from_right, 0, 1)
    far_z_top = shift_row(from_left[:half], 1, 1)
    far_z_bottom = shift_row(from_right[half:], -1, 1)
    return [own, from_z, from_right, from_left], [right_z, far, left_z, far_z_top, far_z_bottom]


def add(*values):
    total = values[0].astype(jnp.float32)
    for value in values[1:]:
        total = total + value.astype(jnp.float32)
    return total


def scatter_col(send, keep):
    got = shift_col(send, 0, 0, 1)

    def pair(dy, dz, *more):
        at = dy * 2 + dz
        return add(keep[at], got[at], *more)

    def send(value, dy, dz):
        return shift_col(value.astype(jnp.bfloat16), dy, dz, 0)

    far_up = send(pair(2, 0), 1, 0)
    far_down = send(pair(2, 1), -1, 0)
    direct_up = send(pair(1, 1), 1, 1)
    direct_down = send(pair(3, 0), -1, 0)
    other = send(pair(0, 1), 0, 1)
    relay_up = send(pair(1, 0, far_up), 1, 0)
    relay_down = send(pair(3, 1, far_down), -1, 1)
    return pair(0, 0, relay_up, relay_down, direct_up, direct_down, other)


def params(mib):
    return pltpu.CompilerParams(vmem_limit_bytes=mib * 1024 * 1024)


any_spec = pl.BlockSpec(memory_space=pl.ANY)
smem_spec = pl.BlockSpec(memory_space=pltpu.SMEM)
vmem_spec = pl.BlockSpec(memory_space=pltpu.VMEM)


def preload_kernel(source, target, sem):
    copy = pltpu.make_async_copy(source, target, sem)
    copy.start()
    copy.wait()


def preload(vals):
    return pl.pallas_call(
        preload_kernel,
        out_shape=pltpu.VMEM(vals.shape, vals.dtype),
        in_specs=[pl.BlockSpec(memory_space=pltpu.HBM)],
        out_specs=vmem_spec,
        scratch_shapes=[pltpu.SemaphoreType.DMA(())],
        compiler_params=params(16),
        cost_estimate=pl.CostEstimate(flops=0, bytes_accessed=2 * vals.size, transcendentals=0),
        name="load_blocks",
    )(pltpu.with_memory_space_constraint(vals, pltpu.HBM))


def start_panel(pieces, panel, sems):
    copies = []
    start = 0
    for index, piece in enumerate(pieces):
        where = panel.at[pl.ds(start, piece.shape[0]), :, pl.ds(0, piece.shape[2])]
        copies.append(pltpu.make_async_copy(piece, where, sems.at[index]))
        start += piece.shape[0]
    for copy in copies:
        copy.start()
    return copies


def product_kernel(section, n_pieces, count_ref, first_ref, second_ref, vals, *refs):
    pieces = refs[:n_pieces]
    refs = refs[n_pieces:]
    last = section >= 1
    if section > 0:
        refs = refs[1:]
    total = refs[0]
    refs = refs[1:]
    if last:
        out_ref, refs = refs[0], refs[1:]
    panel, sems = refs[:2]
    width = pieces[0].shape[2]
    with_degree = panel.shape[2] > width
    zero_block = panel.shape[0] - 1

    copies = start_panel(pieces, panel, sems)
    panel[zero_block] = jnp.zeros(panel.shape[1:], panel.dtype)
    if with_degree:

        @pl.loop(0, zero_block)
        def _(block):
            panel[block, :, width:] = jnp.ones((BLK, panel.shape[2] - width), panel.dtype)

    if section == 0:

        @pl.loop(0, total.shape[0])
        def _(block):
            total[block] = jnp.zeros(total.shape[1:], jnp.float32)

    for copy in copies:
        copy.wait()

    @pl.loop(0, (count_ref[section] + UNROLL - 1) // UNROLL)
    def _(group):
        for u in range(UNROLL):
            first = first_ref[section, group * UNROLL + u]
            second = second_ref[section, group * UNROLL + u]
            row = lax.shift_right_logical(first, 14)
            col_a = lax.shift_right_logical(first, 9) & 31
            col_b = jnp.minimum(lax.shift_right_logical(second, 9) & 31, zero_block)
            col_a = jnp.minimum(col_a, zero_block)
            left = jnp.concatenate([vals[first & 511], vals[second & 511]], axis=1)
            right = jnp.concatenate([panel[col_a], panel[col_b]], axis=0)
            total[row] += jnp.dot(left, right, preferred_element_type=jnp.float32)

    if not last:
        return
    base = (section - 1) * HALF_BLOCKS
    if with_degree:
        degree = refs[2]
        degree[...] = jnp.zeros(degree.shape, jnp.float32)
        eye = lax.broadcasted_iota(jnp.int32, (BLK, BLK), 0) == lax.broadcasted_iota(
            jnp.int32, (BLK, BLK), 1
        )

    @pl.loop(0, DEST)
    def _(dest):
        for j in range(DEV_BLOCKS):
            block = base + dest * DEV_BLOCKS + j
            out_ref[dest, pl.ds(j * BLK, BLK), :] = total[block, :, :width].astype(out_ref.dtype)
            if with_degree:
                spread = jnp.where(eye, total[block, :, width:], 0.0)
                degree[j : j + 1, :] = jnp.sum(spread, axis=0, keepdims=True)
        if with_degree:
            out_ref[dest, pl.ds(DEV_BLOCKS * BLK, 16), :] = degree[...].astype(out_ref.dtype)


def product(plan, vals, hop, total, section, with_degree):
    pieces = [piece.reshape(-1, BLK, piece.shape[-1]) for piece in hop]
    blocks = sum(piece.shape[0] for piece in pieces)
    width = pieces[0].shape[2]
    wide = width + (BLK if with_degree else 0)
    out_shape = [pltpu.VMEM((2 * HALF_BLOCKS, BLK, wide), jnp.float32)]
    scratch = [
        pltpu.VMEM((blocks + 1, BLK, wide), jnp.bfloat16),
        pltpu.SemaphoreType.DMA((len(pieces),)),
    ]
    operands = [*plan, vals, *pieces]
    in_specs = [smem_spec] * 3 + [vmem_spec] + [any_spec] * len(pieces)
    aliases = {}
    if section > 0:
        aliases = {len(operands): 0}
        operands.append(total)
        in_specs.append(vmem_spec)
    if section >= 1:
        rows = DEV_BLOCKS * BLK + (16 if with_degree else 0)
        out_shape.append(jax.ShapeDtypeStruct((DEST, rows, width), jnp.bfloat16))
        if with_degree:
            scratch.append(pltpu.VMEM((16, BLK), jnp.float32))
    flops = (6_000_000_000, 3_000_000_000, 3_000_000_000)[section]
    return pl.pallas_call(
        functools.partial(product_kernel, section, len(pieces)),
        out_shape=out_shape,
        in_specs=in_specs,
        out_specs=[vmem_spec] * len(out_shape),
        scratch_shapes=scratch,
        input_output_aliases=aliases,
        compiler_params=params(16),
        cost_estimate=pl.CostEstimate(flops=flops, bytes_accessed=1 << 20, transcendentals=0),
        name=("product_near", "product_send", "product_keep")[section],
    )(*operands)


def layer_product(plan, vals, hops, with_degree):
    (total,) = product(plan, vals, hops[0], None, 0, with_degree)
    total, send = product(plan, vals, hops[1], total, 1, with_degree)
    total, keep = product(plan, vals, hops[1], total, 2, with_degree)
    return send, keep


def score_kernel(n_pieces, pair_ref, own, target, attributes, w_attr, attr_bias, *refs):
    pieces = refs[:n_pieces]
    out_ref, panel, sems = refs[n_pieces:]
    copies = start_panel(pieces, panel, sems)
    scale = own.shape[1] ** (-0.5)
    n_pair = pair_ref.shape[1]

    def row_mean(squares, count):
        return jnp.sum(squares.T, axis=0, keepdims=True) / count

    errors = []
    for block in range(DEV_BLOCKS):
        rows = pl.ds(block * BLK, BLK)
        rebuilt = jnp.dot(own[rows, :], w_attr[...], preferred_element_type=jnp.float32)
        gap = rebuilt + attr_bias[...] - attributes[rows, :].astype(jnp.float32)
        errors.append(jnp.sqrt(row_mean(gap * gap, gap.shape[1]) + epsilon))
    for copy in copies:
        copy.wait()
    for block in range(DEV_BLOCKS):
        rows = pl.ds(block * BLK, BLK)
        squares = jnp.zeros((BLK, BLK), jnp.float32)
        for pair in range(n_pair):
            logits = lax.dot_general(
                own[rows, :],
                panel[pair_ref[block, pair]],
                (((1,), (1,)), ((), ())),
                preferred_element_type=jnp.float32,
            )
            gap = jax.nn.sigmoid(logits * scale) - target[rows, pl.ds(pair * BLK, BLK)].astype(
                jnp.float32
            )
            squares = squares + gap * gap
        struct = jnp.sqrt(row_mean(squares, n_pair * BLK) + epsilon)
        out_ref[block : block + 1, :] = mix_alpha * errors[block] + (1.0 - mix_alpha) * struct


def score(hops, pairs, own, target, attributes, w_attr, attr_bias):
    pieces = [piece.reshape(-1, BLK, piece.shape[-1]) for hop in hops for piece in hop]
    out = pl.pallas_call(
        functools.partial(score_kernel, len(pieces)),
        out_shape=jax.ShapeDtypeStruct((DEV_BLOCKS, BLK), jnp.float32),
        in_specs=[smem_spec] + [vmem_spec] * 5 + [any_spec] * len(pieces),
        out_specs=vmem_spec,
        scratch_shapes=[
            pltpu.VMEM((N_ROW * DEV_BLOCKS, BLK, own.shape[1]), jnp.bfloat16),
            pltpu.SemaphoreType.DMA((len(pieces),)),
        ],
        compiler_params=params(16),
        name="score",
    )(pairs, own, target, attributes, w_attr, attr_bias, *pieces)
    return out.reshape(-1)


def make_plan(row_ids, col_ids, live_count, row_at, col_at):
    capacity = row_ids.shape[0]
    sections = 3
    slots = jnp.arange(capacity, dtype=jnp.int32)
    live = slots < live_count
    y, z_hi, core = col_at // 4, (col_at // 2) % 2, col_at % 2
    dest, j = row_ids // DEV_BLOCKS, row_ids % DEV_BLOCKS
    dy = (dest // 4 - y) % N_Y
    dz = (dest // 2 + z_hi) % 2
    keep = 1 - (dest + core) % 2
    row = keep * HALF_BLOCKS + (dy * 2 + dz) * DEV_BLOCKS + j
    hop, col = relative_block(col_ids, row_at)
    section = jnp.where(hop == 1, 1 + keep, 0)
    key = section * (2 * HALF_BLOCKS) + row
    same = (key[:, None] == key[None, :]) & live[None, :]
    within = jnp.sum((same & (slots[None, :] < slots[:, None])).astype(jnp.int32), axis=1)
    opens = live & (within % 2 == 0)
    ahead = (key[None, :] < key[:, None]) & (section[None, :] == section[:, None]) & opens[None, :]
    pair = jnp.sum(ahead.astype(jnp.int32), axis=1) + within // 2
    longest = -(-((capacity + 2 * HALF_BLOCKS) // 2) // UNROLL) * UNROLL
    place = jnp.where(live, (section * longest + pair) * 2 + within % 2, -1)
    places = jnp.arange(sections * longest, dtype=jnp.int32)
    empty = 31 * 512
    word = slots + col * 512 + row * (512 * 32) - empty

    def lay(side):
        hit = place[None, :] == (places * 2 + side)[:, None]
        found = jnp.sum(jnp.where(hit, word[None, :], 0), axis=1)
        return (empty + found).reshape(sections, longest)

    count = jnp.sum(
        (opens[None, :] & (section[None, :] == jnp.arange(sections)[:, None])).astype(jnp.int32),
        axis=1,
    )
    return count, lay(0), lay(1)


def relative_block(ids, row_at):
    owner, j = ids // DEV_BLOCKS, ids % DEV_BLOCKS
    offset = ((owner // 2 - row_at // 2) % N_X) * 2 + (owner + row_at) % 2
    hop = jnp.zeros_like(ids)
    place = jnp.zeros_like(ids)
    for at in range(N_ROW):
        hop = jnp.where(offset == at, HOP[at], hop)
        place = jnp.where(offset == at, PLACE[at], place)
    return hop, place * DEV_BLOCKS + j


def per_device(
    attributes,
    adj_values,
    adj_rows,
    adj_cols,
    adj_count,
    pair_ids,
    struct_target,
    w_first,
    w_rest,
    layer_bias,
    w_attr,
    attr_bias,
):
    vals = preload(adj_values[0, 0])
    hidden_size = w_rest.shape[1]
    row_at = lax.axis_index("row")
    col_at = lax.axis_index("col")
    plan = make_plan(adj_rows[0, 0], adj_cols[0, 0], adj_count[0, 0], row_at, col_at)
    nodes_dev = attributes.shape[0]
    w_near, w_self = w_first[:, :hidden_size], w_first[:, hidden_size:]
    own_part = jnp.dot(attributes, w_self, preferred_element_type=jnp.float32)

    summed = scatter_col(*layer_product(plan, vals, gather_row(attributes), True))
    degree = 1.0 + summed[nodes_dev : nodes_dev + DEV_BLOCKS].reshape(-1)
    row_scale = lax.rsqrt(degree)[:, None]
    aggregate = summed[:nodes_dev]
    coarse = lax.reduce_precision(aggregate, 8, 7)
    fine = (aggregate - coarse).astype(jnp.bfloat16)
    coarse = coarse.astype(jnp.bfloat16)
    mixed = jnp.dot(coarse, w_near, preferred_element_type=jnp.float32) + jnp.dot(
        fine, w_near, preferred_element_type=jnp.float32
    )
    hidden = jnp.tanh(row_scale * mixed + own_part).astype(jnp.bfloat16)

    features = jnp.dot(
        hidden, w_rest[0][:, :hidden_size], preferred_element_type=jnp.float32
    ).astype(jnp.bfloat16)
    hops = gather_row(features)
    own_part = (
        jnp.dot(hidden, w_rest[0][:, hidden_size:], preferred_element_type=jnp.float32)
        + layer_bias[0]
    )
    summed = scatter_col(*layer_product(plan, vals, hops, False))
    hidden = jnp.tanh(row_scale * summed + own_part).astype(jnp.bfloat16)

    hop, place = relative_block(pair_ids, row_at)
    return score(
        gather_row(hidden),
        hop * (N_ROW // 2) * DEV_BLOCKS + place,
        hidden,
        struct_target.reshape(nodes_dev, -1),
        attributes,
        w_attr,
        attr_bias[None, :],
    )


def solution(mesh):
    return jax.shard_map(
        per_device,
        mesh=mesh,
        in_specs=(
            P(("row", "col"), None),
            P("row", "col", None, None, None),
            P("row", "col", None),
            P("row", "col", None),
            P("row", "col"),
            P(("row", "col"), None),
            P(("row", "col"), None, None),
            P(),
            P(),
            P(),
            P(),
            P(),
        ),
        out_specs=P(("row", "col")),
        check_vma=False,
    )
```

```python
import functools

import jax
import jax.numpy as jnp
from jax import lax
from jax.experimental import pallas as pl
from jax.experimental.pallas import tpu as pltpu
from jax.sharding import PartitionSpec as P

epsilon = 1e-06
mix_alpha = 0.8

BLK = 128
N_X, N_Y = 4, 4
N_ROW, N_COL = 8, 16
DEV_BLOCKS = 4
DEST = 8
HALF_BLOCKS = DEST * DEV_BLOCKS
HOP = (0, 0, 0, 1, 1, 1, 0, 1)
PLACE = (0, 1, 2, 1, 0, 3, 3, 2)
UNROLL = 8
TAKEN = 4
STEPS = 256
EMPTY = 31 * 512


def row_of(x, z_lo):
    return (x % N_X) * 2 + z_lo


def col_of(y, z_hi, core):
    return ((y % N_Y) * 2 + z_hi) * 2 + core


def shift_row(value, dx, dz):
    perm = [(row_of(x, z), row_of(x + dx, z ^ dz)) for x in range(N_X) for z in range(2)]
    return lax.ppermute(value, "row", perm)


def shift_col(value, dy, dz, dc):
    perm = [
        (col_of(y, z, c), col_of(y + dy, z ^ dz, c ^ dc))
        for y in range(N_Y)
        for z in range(2)
        for c in range(2)
    ]
    return lax.ppermute(value, "col", perm)


def gather_row(own, joined):
    from_left = shift_row(own, 1, 0)
    from_right = shift_row(own, -1, 0)
    from_z = shift_row(own, 0, 1)
    near = [own, from_z, from_right, from_left]
    left_z = shift_row(from_z, 1, 0)
    if joined:
        far_right_z = shift_row(jnp.concatenate([from_right, from_z]), -1, 0)
        far_z = shift_row(from_left, 1, 1)
        return near, [far_right_z, left_z, far_z]
    half = own.shape[0] // 2
    far = shift_row(from_right, -1, 0)
    right_z = shift_row(from_right, 0, 1)
    far_z_top = shift_row(from_left[:half], 1, 1)
    far_z_bottom = shift_row(from_right[half:], -1, 1)
    return near, [far, right_z, left_z, far_z_top, far_z_bottom]


def add(*values):
    total = values[0].astype(jnp.float32)
    for value in values[1:]:
        total = total + value.astype(jnp.float32)
    return total


def scatter_col(send, keep):
    got = shift_col(send, 0, 0, 1)

    def pair(dy, dz, *more):
        at = dy * 2 + dz
        return add(keep[at], got[at], *more)

    def send(value, dy, dz):
        return shift_col(value.astype(jnp.bfloat16), dy, dz, 0)

    far_up = send(pair(2, 0), 1, 0)
    far_down = send(pair(2, 1), -1, 0)
    direct_up = send(pair(1, 1), 1, 1)
    direct_down = send(pair(3, 0), -1, 0)
    other = send(pair(0, 1), 0, 1)
    relay_up = send(pair(1, 0, far_up), 1, 0)
    relay_down = send(pair(3, 1, far_down), -1, 1)
    return pair(0, 0, relay_up, relay_down, direct_up, direct_down, other)


def params(mib):
    return pltpu.CompilerParams(vmem_limit_bytes=mib * 1024 * 1024)


any_spec = pl.BlockSpec(memory_space=pl.ANY)
smem_spec = pl.BlockSpec(memory_space=pltpu.SMEM)
vmem_spec = pl.BlockSpec(memory_space=pltpu.VMEM)


def down(row):
    return jnp.broadcast_to(row.astype(jnp.float32), (BLK, row.shape[1])).T


def clear(total):
    @pl.loop(0, total.shape[0])
    def _(block):
        total[block] = jnp.zeros(total.shape[1:], jnp.float32)


def begin_kernel(place_ref, rows_ref, cols_ref, source, vals, total, plan, sem):
    copy = pltpu.make_async_copy(source, vals, sem)
    copy.start()
    count, row_at, col_at = place_ref[0], place_ref[1], place_ref[2]
    y, z_hi, core = col_at >> 2, (col_at >> 1) & 1, col_at & 1
    rows = rows_ref[...]
    capacity = rows.shape[1]
    slots = lax.broadcasted_iota(jnp.int32, rows.shape, 1)
    live = slots < count
    dest, j = rows >> 2, rows & 3
    dy = ((dest >> 2) - y) & 3
    dz = ((dest >> 1) + z_hi) & 1
    keep = 1 - ((dest + core) & 1)
    row = keep * HALF_BLOCKS + (dy * 2 + dz) * DEV_BLOCKS + j
    hop, col = relative_block(cols_ref[...], row_at)
    section = jnp.where(hop == 1, 1 + keep, 0)
    key = jnp.where(live, section * (2 * HALF_BLOCKS) + row, 1024).astype(jnp.float32)
    parts = capacity // BLK
    square = (capacity, capacity)
    earlier = lax.broadcasted_iota(jnp.int32, square, 0) < lax.broadcasted_iota(jnp.int32, square, 1)

    def wide(column):
        return jnp.concatenate([column] * parts, axis=1)

    def tally(mask):
        return jnp.sum(jnp.where(mask, 1.0, 0.0), axis=0, keepdims=True)

    within = tally((wide(down(key)) == key) & earlier).astype(jnp.int32)
    opens = live & ((within & (TAKEN - 1)) == 0)
    opener = wide(down(jnp.where(opens, key, 2048.0)))
    least = (section * (2 * HALF_BLOCKS)).astype(jnp.float32)
    step = tally((opener >= least) & (opener < key)).astype(jnp.int32) + within // TAKEN
    lane = lax.broadcasted_iota(jnp.int32, (1, STEPS), 1)
    ends = jnp.zeros((1, 1), jnp.int32)
    begin = jnp.zeros(rows.shape, jnp.int32)
    bounds = jnp.zeros((1, STEPS), jnp.int32)
    for kind in range(3):
        begin = jnp.where(section == kind, ends, begin)
        mine = jnp.where(opens & (section == kind), 1.0, 0.0)
        number = jnp.sum(mine, axis=1, keepdims=True).astype(jnp.int32)
        ends = ends + (number + UNROLL - 1) // UNROLL
        bounds = jnp.where(lane == kind + 1, ends, bounds)
    spot = (begin * UNROLL + step) * TAKEN + (within & (TAKEN - 1))
    spot = down(jnp.where(live, spot, -1))
    word = down(slots + col * 512 + row * (512 * 32) - EMPTY)
    for side in range(TAKEN):
        for part in range(STEPS // BLK):
            here = lax.broadcasted_iota(jnp.int32, (1, BLK), 1) + part * BLK
            hit = spot == (here * TAKEN + side).astype(jnp.float32)
            found = jnp.sum(jnp.where(hit, word, 0.0), axis=0, keepdims=True)
            plan[side : side + 1, part * BLK : (part + 1) * BLK] = found.astype(jnp.int32) + EMPTY
    plan[TAKEN : TAKEN + 1, :] = bounds
    clear(total)
    copy.wait()


total_shape = (2 * HALF_BLOCKS, BLK, 2 * BLK)


def begin(vals, row_ids, col_ids, live_count, row_at, col_at):
    place = jnp.stack([live_count, row_at, col_at]).astype(jnp.int32)
    return pl.pallas_call(
        begin_kernel,
        out_shape=[
            pltpu.VMEM(vals.shape, vals.dtype),
            pltpu.VMEM(total_shape, jnp.float32),
            jax.ShapeDtypeStruct((TAKEN + 1, STEPS), jnp.int32),
        ],
        in_specs=[smem_spec, vmem_spec, vmem_spec, pl.BlockSpec(memory_space=pltpu.HBM)],
        out_specs=[vmem_spec] * 3,
        scratch_shapes=[pltpu.SemaphoreType.DMA(())],
        compiler_params=params(16),
        cost_estimate=pl.CostEstimate(flops=0, bytes_accessed=2 * vals.size, transcendentals=0),
        name="begin",
    )(
        place,
        row_ids[None, :],
        col_ids[None, :],
        pltpu.with_memory_space_constraint(vals, pltpu.HBM),
    )


def cleared(after):
    return pl.pallas_call(
        lambda after_ref, total: clear(total),
        out_shape=pltpu.VMEM(total_shape, jnp.float32),
        in_specs=[any_spec],
        out_specs=vmem_spec,
        compiler_params=params(16),
        cost_estimate=pl.CostEstimate(flops=0, bytes_accessed=1 << 21, transcendentals=0),
        name="cleared",
    )(after)


def start_panel(pieces, panel, sems):
    copies = []
    start = 0
    for index, piece in enumerate(pieces):
        where = panel.at[pl.ds(start, piece.shape[0]), :, pl.ds(0, piece.shape[2])]
        copies.append(pltpu.make_async_copy(piece, where, sems.at[index]))
        start += piece.shape[0]
    for copy in copies:
        copy.start()
    return copies


def product_kernel(section, n_pieces, plan, vals, *refs):
    pieces = refs[:n_pieces]
    refs = refs[n_pieces:]
    last = section >= 1
    total, refs = refs[1], refs[2:]
    if last:
        out_ref, refs = refs[0], refs[1:]
    panel, sems = refs[:2]
    width = pieces[0].shape[2]
    with_degree = panel.shape[2] > width
    zero_block = panel.shape[0] - 1

    copies = start_panel(pieces, panel, sems)
    panel[zero_block] = jnp.zeros(panel.shape[1:], panel.dtype)
    if with_degree:

        @pl.loop(0, zero_block)
        def _(block):
            panel[block, :, width:] = jnp.ones((BLK, panel.shape[2] - width), panel.dtype)

    for copy in copies:
        copy.wait()

    @pl.loop(plan[TAKEN, section], plan[TAKEN, section + 1])
    def _(group):
        for u in range(UNROLL):
            words = [plan[side, group * UNROLL + u] for side in range(TAKEN)]
            cols = [jnp.minimum((word >> 9) & 31, zero_block) for word in words]
            left = jnp.concatenate([vals[word & 511] for word in words], axis=1)
            right = jnp.concatenate([panel[col] for col in cols], axis=0)
            row = words[0] >> 14
            total[row] += jnp.dot(left, right, preferred_element_type=jnp.float32)

    if not last:
        return
    base = (section - 1) * HALF_BLOCKS
    if with_degree:
        degree = refs[2]
        degree[...] = jnp.zeros(degree.shape, jnp.float32)
        eye = lax.broadcasted_iota(jnp.int32, (BLK, BLK), 0) == lax.broadcasted_iota(
            jnp.int32, (BLK, BLK), 1
        )

    @pl.loop(0, DEST)
    def _(dest):
        for j in range(DEV_BLOCKS):
            block = base + dest * DEV_BLOCKS + j
            out_ref[dest, pl.ds(j * BLK, BLK), :] = total[block, :, :width].astype(out_ref.dtype)
            if with_degree:
                spread = jnp.where(eye, total[block, :, width:], 0.0)
                degree[j : j + 1, :] = jnp.sum(spread, axis=0, keepdims=True)
        if with_degree:
            out_ref[dest, pl.ds(DEV_BLOCKS * BLK, 16), :] = degree[...].astype(out_ref.dtype)


def product(plan, vals, hop, total, section, with_degree):
    pieces = [piece.reshape(-1, BLK, piece.shape[-1]) for piece in hop]
    blocks = sum(piece.shape[0] for piece in pieces)
    width = pieces[0].shape[2]
    wide = width + (BLK if with_degree else 0)
    out_shape = [pltpu.VMEM(total_shape, jnp.float32)]
    scratch = [
        pltpu.VMEM((blocks + 1, BLK, wide), jnp.bfloat16),
        pltpu.SemaphoreType.DMA((len(pieces),)),
    ]
    operands = [plan, vals, *pieces, total]
    in_specs = [smem_spec, vmem_spec] + [any_spec] * len(pieces) + [vmem_spec]
    aliases = {len(operands) - 1: 0}
    if section >= 1:
        rows = DEV_BLOCKS * BLK + (16 if with_degree else 0)
        out_shape.append(jax.ShapeDtypeStruct((DEST, rows, width), jnp.bfloat16))
        if with_degree:
            scratch.append(pltpu.VMEM((16, BLK), jnp.float32))
    flops = (6_000_000_000, 3_000_000_000, 3_000_000_000)[section]
    return pl.pallas_call(
        functools.partial(product_kernel, section, len(pieces)),
        out_shape=out_shape,
        in_specs=in_specs,
        out_specs=[vmem_spec] * len(out_shape),
        scratch_shapes=scratch,
        input_output_aliases=aliases,
        compiler_params=params(16),
        cost_estimate=pl.CostEstimate(flops=flops, bytes_accessed=1 << 20, transcendentals=0),
        name=("product_near", "product_send", "product_keep")[section],
    )(*operands)


def layer_product(plan, vals, total, hops, with_degree):
    (total,) = product(plan, vals, hops[0], total, 0, with_degree)
    total, send = product(plan, vals, hops[1], total, 1, with_degree)
    total, keep = product(plan, vals, hops[1], total, 2, with_degree)
    return send, keep


def score_kernel(n_pieces, pair_ref, own, target, attributes, w_attr, attr_bias, *refs):
    pieces = refs[:n_pieces]
    out_ref, panel, sems = refs[n_pieces:]
    copies = start_panel(pieces, panel, sems)
    scale = own.shape[1] ** (-0.5)
    n_pair = pair_ref.shape[1]

    def row_mean(squares, count):
        return jnp.sum(squares.T, axis=0, keepdims=True) / count

    errors = []
    for block in range(DEV_BLOCKS):
        rows = pl.ds(block * BLK, BLK)
        rebuilt = jnp.dot(own[rows, :], w_attr[...], preferred_element_type=jnp.float32)
        gap = rebuilt + attr_bias[...] - attributes[rows, :].astype(jnp.float32)
        errors.append(jnp.sqrt(row_mean(gap * gap, gap.shape[1]) + epsilon))
    for copy in copies:
        copy.wait()
    for block in range(DEV_BLOCKS):
        rows = pl.ds(block * BLK, BLK)
        squares = jnp.zeros((BLK, BLK), jnp.float32)
        for pair in range(n_pair):
            logits = lax.dot_general(
                own[rows, :],
                panel[pair_ref[block, pair]],
                (((1,), (1,)), ((), ())),
                preferred_element_type=jnp.float32,
            )
            gap = jax.nn.sigmoid(logits * scale) - target[rows, pl.ds(pair * BLK, BLK)].astype(
                jnp.float32
            )
            squares = squares + gap * gap
        struct = jnp.sqrt(row_mean(squares, n_pair * BLK) + epsilon)
        out_ref[block : block + 1, :] = mix_alpha * errors[block] + (1.0 - mix_alpha) * struct


def score(hops, pairs, own, target, attributes, w_attr, attr_bias):
    pieces = [piece.reshape(-1, BLK, piece.shape[-1]) for hop in hops for piece in hop]
    out = pl.pallas_call(
        functools.partial(score_kernel, len(pieces)),
        out_shape=jax.ShapeDtypeStruct((DEV_BLOCKS, BLK), jnp.float32),
        in_specs=[smem_spec] + [vmem_spec] * 5 + [any_spec] * len(pieces),
        out_specs=vmem_spec,
        scratch_shapes=[
            pltpu.VMEM((N_ROW * DEV_BLOCKS, BLK, own.shape[1]), jnp.bfloat16),
            pltpu.SemaphoreType.DMA((len(pieces),)),
        ],
        compiler_params=params(16),
        name="score",
    )(pairs, own, target, attributes, w_attr, attr_bias, *pieces)
    return out.reshape(-1)


def relative_block(ids, row_at):
    owner = ids >> 2
    offset = (((owner >> 1) - (row_at >> 1)) & 3) * 2 + ((owner + row_at) & 1)
    hop = jnp.zeros_like(ids)
    place = jnp.zeros_like(ids)
    for at in range(N_ROW):
        hop = jnp.where(offset == at, HOP[at], hop)
        place = jnp.where(offset == at, PLACE[at], place)
    return hop, place * DEV_BLOCKS + (ids & 3)


def per_device(
    attributes,
    adj_values,
    adj_rows,
    adj_cols,
    adj_count,
    pair_ids,
    struct_target,
    w_first,
    w_rest,
    layer_bias,
    w_attr,
    attr_bias,
):
    hidden_size = w_rest.shape[1]
    row_at = lax.axis_index("row")
    col_at = lax.axis_index("col")
    vals, total, plan = begin(
        adj_values[0, 0], adj_rows[0, 0], adj_cols[0, 0], adj_count[0, 0], row_at, col_at
    )
    nodes_dev = attributes.shape[0]
    w_near, w_self = w_first[:, :hidden_size], w_first[:, hidden_size:]
    own_part = jnp.dot(attributes, w_self, preferred_element_type=jnp.float32)

    send, keep = layer_product(plan, vals, total, gather_row(attributes, True), True)
    summed = scatter_col(send, keep)
    degree = 1.0 + summed[nodes_dev : nodes_dev + DEV_BLOCKS].reshape(-1)
    row_scale = lax.rsqrt(degree)[:, None]
    aggregate = summed[:nodes_dev]
    coarse = lax.reduce_precision(aggregate, 8, 7)
    fine = (aggregate - coarse).astype(jnp.bfloat16)
    coarse = coarse.astype(jnp.bfloat16)
    mixed = jnp.dot(coarse, w_near, preferred_element_type=jnp.float32) + jnp.dot(
        fine, w_near, preferred_element_type=jnp.float32
    )
    hidden = jnp.tanh(row_scale * mixed + own_part).astype(jnp.bfloat16)

    features = jnp.dot(
        hidden, w_rest[0][:, :hidden_size], preferred_element_type=jnp.float32
    ).astype(jnp.bfloat16)
    hops = gather_row(features, True)
    own_part = (
        jnp.dot(hidden, w_rest[0][:, hidden_size:], preferred_element_type=jnp.float32)
        + layer_bias[0]
    )
    summed = scatter_col(*layer_product(plan, vals, cleared(keep), hops, False))
    hidden = jnp.tanh(row_scale * summed + own_part).astype(jnp.bfloat16)

    hop, place = relative_block(pair_ids, row_at)
    return score(
        gather_row(hidden, False),
        hop * (N_ROW // 2) * DEV_BLOCKS + place,
        hidden,
        struct_target.reshape(nodes_dev, -1),
        attributes,
        w_attr,
        attr_bias[None, :],
    )


def solution(mesh):
    return jax.shard_map(
        per_device,
        mesh=mesh,
        in_specs=(
            P(("row", "col"), None),
            P("row", "col", None, None, None),
            P("row", "col", None),
            P("row", "col", None),
            P("row", "col"),
            P(("row", "col"), None),
            P(("row", "col"), None, None),
            P(),
            P(),
            P(),
            P(),
            P(),
        ),
        out_specs=P(("row", "col")),
        check_vma=False,
    )
```

```python
import functools

import jax
import jax.numpy as jnp
from jax import lax
from jax.experimental import pallas as pl
from jax.experimental.pallas import tpu as pltpu
from jax.sharding import PartitionSpec as P

epsilon = 1e-06
mix_alpha = 0.8

BLK = 128
N_X, N_Y = 4, 4
N_ROW, N_COL = 8, 16
DEV_BLOCKS = 4
DEST = 8
HALF_BLOCKS = DEST * DEV_BLOCKS
HOP = (0, 0, 0, 1, 1, 1, 0, 1)
PLACE = (0, 1, 2, 1, 0, 3, 3, 2)
UNROLL = (16, 8, 8)
TAKEN = 4
STEPS = 256
EMPTY = 31 * 512


def row_of(x, z_lo):
    return (x % N_X) * 2 + z_lo


def col_of(y, z_hi, core):
    return ((y % N_Y) * 2 + z_hi) * 2 + core


def shift_row(value, dx, dz):
    perm = [(row_of(x, z), row_of(x + dx, z ^ dz)) for x in range(N_X) for z in range(2)]
    return lax.ppermute(value, "row", perm)


def shift_col(value, dy, dz, dc):
    perm = [
        (col_of(y, z, c), col_of(y + dy, z ^ dz, c ^ dc))
        for y in range(N_Y)
        for z in range(2)
        for c in range(2)
    ]
    return lax.ppermute(value, "col", perm)


def gather_row(own, joined):
    from_left = shift_row(own, 1, 0)
    from_right = shift_row(own, -1, 0)
    from_z = shift_row(own, 0, 1)
    near = [own, from_z, from_right, from_left]
    left_z = shift_row(from_z, 1, 0)
    if joined:
        far_right_z = shift_row(jnp.concatenate([from_right, from_z]), -1, 0)
        far_z = shift_row(from_left, 1, 1)
        return near, [far_right_z, left_z, far_z]
    far_z = shift_row(from_left, 1, 1)
    far = shift_row(from_right, -1, 0)
    right_z = shift_row(from_right, 0, 1)
    return near, [far, right_z, left_z, far_z]


def add(*values):
    total = values[0].astype(jnp.float32)
    for value in values[1:]:
        total = total + value.astype(jnp.float32)
    return total


def scatter_col(send, keep):
    got = shift_col(send, 0, 0, 1)

    def pair(dy, dz, *more):
        at = dy * 2 + dz
        return add(keep[at], got[at], *more)

    def send(value, dy, dz):
        return shift_col(value.astype(jnp.bfloat16), dy, dz, 0)

    other = send(pair(0, 1), 0, 1)
    far_down = send(pair(2, 1), -1, 0)
    far_up = send(pair(2, 0), 1, 0)
    other, far_down, far_up = lax.optimization_barrier((other, far_down, far_up))
    direct_up = send(pair(1, 1), 1, 1)
    relay_down = send(pair(3, 1, far_down), -1, 1)
    relay_up = send(pair(1, 0, far_up), 1, 0)
    direct_down = send(pair(3, 0), -1, 0)
    return pair(0, 0, other, direct_up, relay_down, relay_up, direct_down)


def params(mib):
    return pltpu.CompilerParams(vmem_limit_bytes=mib * 1024 * 1024)


any_spec = pl.BlockSpec(memory_space=pl.ANY)
smem_spec = pl.BlockSpec(memory_space=pltpu.SMEM)
vmem_spec = pl.BlockSpec(memory_space=pltpu.VMEM)


def down(row):
    return jnp.broadcast_to(row.astype(jnp.float32), (BLK, row.shape[1])).T


def clear(total):
    @pl.loop(0, total.shape[0])
    def _(block):
        total[block] = jnp.zeros(total.shape[1:], jnp.float32)


def begin_kernel(place_ref, rows_in, cols_in, source, vals, total, plan, lists, sem, list_sem):
    copy = pltpu.make_async_copy(source, vals, sem)
    list_copies = [
        pltpu.make_async_copy(ids, lists.at[at], list_sem.at[at])
        for at, ids in enumerate((rows_in, cols_in))
    ]
    for list_copy in list_copies:
        list_copy.start()
    copy.start()
    for list_copy in list_copies:
        list_copy.wait()
    count, row_at, col_at = place_ref[0], place_ref[1], place_ref[2]
    y, z_hi, core = col_at >> 2, (col_at >> 1) & 1, col_at & 1
    rows = lists[0]
    capacity = rows.shape[1]
    slots = lax.broadcasted_iota(jnp.int32, rows.shape, 1)
    live = slots < count
    dest, j = rows >> 2, rows & 3
    dy = ((dest >> 2) - y) & 3
    dz = ((dest >> 1) + z_hi) & 1
    keep = 1 - ((dest + core) & 1)
    row = keep * HALF_BLOCKS + (dy * 2 + dz) * DEV_BLOCKS + j
    hop, col = relative_block(lists[1], row_at)
    section = jnp.where(hop == 1, 1 + keep, 0)
    key = jnp.where(live, section * (2 * HALF_BLOCKS) + row, 1024).astype(jnp.float32)
    parts = capacity // BLK
    square = (capacity, capacity)
    earlier = lax.broadcasted_iota(jnp.int32, square, 0) < lax.broadcasted_iota(jnp.int32, square, 1)

    def wide(column):
        return jnp.concatenate([column] * parts, axis=1)

    def tally(mask):
        return jnp.sum(jnp.where(mask, 1.0, 0.0), axis=0, keepdims=True)

    within = tally((wide(down(key)) == key) & earlier).astype(jnp.int32)
    opens = live & ((within & (TAKEN - 1)) == 0)
    opener = wide(down(jnp.where(opens, key, 2048.0)))
    least = (section * (2 * HALF_BLOCKS)).astype(jnp.float32)
    step = tally((opener >= least) & (opener < key)).astype(jnp.int32) + within // TAKEN
    lane = lax.broadcasted_iota(jnp.int32, (1, STEPS), 1)
    ends = jnp.zeros((1, 1), jnp.int32)
    begin = jnp.zeros(rows.shape, jnp.int32)
    bounds = jnp.zeros((1, STEPS), jnp.int32)
    for kind in range(3):
        begin = jnp.where(section == kind, ends, begin)
        mine = jnp.where(opens & (section == kind), 1.0, 0.0)
        number = jnp.sum(mine, axis=1, keepdims=True).astype(jnp.int32)
        groups = (number + UNROLL[kind] - 1) // UNROLL[kind]
        ends = ends + groups * UNROLL[kind]
        bounds = jnp.where(lane == kind + 1, ends, bounds)
    spot = (begin + step) * TAKEN + (within & (TAKEN - 1))
    spot = down(jnp.where(live, spot, -1))
    word = down(slots + col * 512 + row * (512 * 32) - EMPTY)
    for side in range(TAKEN):
        for part in range(STEPS // BLK):
            here = lax.broadcasted_iota(jnp.int32, (1, BLK), 1) + part * BLK
            hit = spot == (here * TAKEN + side).astype(jnp.float32)
            found = jnp.sum(jnp.where(hit, word, 0.0), axis=0, keepdims=True)
            plan[side : side + 1, part * BLK : (part + 1) * BLK] = found.astype(jnp.int32) + EMPTY
    plan[TAKEN : TAKEN + 1, :] = bounds
    clear(total)
    copy.wait()


total_shape = (2 * HALF_BLOCKS, BLK, 2 * BLK)


def begin(vals, row_ids, col_ids, live_count, row_at, col_at):
    place = jnp.stack([live_count, row_at, col_at]).astype(jnp.int32)
    return pl.pallas_call(
        begin_kernel,
        out_shape=[
            pltpu.VMEM(vals.shape, vals.dtype),
            pltpu.VMEM(total_shape, jnp.float32),
            jax.ShapeDtypeStruct((TAKEN + 1, STEPS), jnp.int32),
        ],
        in_specs=[smem_spec] + [pl.BlockSpec(memory_space=pltpu.HBM)] * 3,
        out_specs=[vmem_spec] * 3,
        scratch_shapes=[
            pltpu.VMEM((2, 1, row_ids.shape[0]), jnp.int32),
            pltpu.SemaphoreType.DMA(()),
            pltpu.SemaphoreType.DMA((2,)),
        ],
        compiler_params=params(16),
        cost_estimate=pl.CostEstimate(flops=0, bytes_accessed=2 * vals.size, transcendentals=0),
        name="begin",
    )(
        place,
        pltpu.with_memory_space_constraint(row_ids[None, :], pltpu.HBM),
        pltpu.with_memory_space_constraint(col_ids[None, :], pltpu.HBM),
        pltpu.with_memory_space_constraint(vals, pltpu.HBM),
    )


def cleared(after):
    return pl.pallas_call(
        lambda after_ref, total: clear(total),
        out_shape=pltpu.VMEM(total_shape, jnp.float32),
        in_specs=[any_spec],
        out_specs=vmem_spec,
        compiler_params=params(16),
        cost_estimate=pl.CostEstimate(flops=0, bytes_accessed=1 << 21, transcendentals=0),
        name="cleared",
    )(after)


def start_panel(pieces, panel, sems):
    copies = []
    start = 0
    for index, piece in enumerate(pieces):
        where = panel.at[pl.ds(start, piece.shape[0]), :, pl.ds(0, piece.shape[2])]
        copies.append(pltpu.make_async_copy(piece, where, sems.at[index]))
        start += piece.shape[0]
    for copy in copies:
        copy.start()
    return copies


def product_kernel(section, n_pieces, plan, vals, *refs):
    pieces = refs[:n_pieces]
    refs = refs[n_pieces:]
    last = section >= 1
    total, refs = refs[1], refs[2:]
    if last:
        out_ref, refs = refs[0], refs[1:]
    panel, sems = refs[:2]
    width = pieces[0].shape[2]
    with_degree = panel.shape[2] > width
    zero_block = panel.shape[0] - 1

    copies = start_panel(pieces, panel, sems)
    panel[zero_block] = jnp.zeros(panel.shape[1:], panel.dtype)
    if with_degree:

        @pl.loop(0, zero_block)
        def _(block):
            panel[block, :, width:] = jnp.ones((BLK, panel.shape[2] - width), panel.dtype)

    for copy in copies:
        copy.wait()

    @pl.loop(plan[TAKEN, section], plan[TAKEN, section + 1], step=UNROLL[section])
    def _(group):
        for u in range(UNROLL[section]):
            words = [plan[side, group + u] for side in range(TAKEN)]
            cols = [jnp.minimum((word >> 9) & 31, zero_block) for word in words]
            left = jnp.concatenate([vals[word & 511] for word in words], axis=1)
            right = jnp.concatenate([panel[col] for col in cols], axis=0)
            row = words[0] >> 14
            total[row] += jnp.dot(left, right, preferred_element_type=jnp.float32)

    if not last:
        return
    base = (section - 1) * HALF_BLOCKS
    if with_degree:
        degree = refs[2]
        degree[...] = jnp.zeros(degree.shape, jnp.float32)
        eye = lax.broadcasted_iota(jnp.int32, (BLK, BLK), 0) == lax.broadcasted_iota(
            jnp.int32, (BLK, BLK), 1
        )

    @pl.loop(0, DEST)
    def _(dest):
        for j in range(DEV_BLOCKS):
            block = base + dest * DEV_BLOCKS + j
            out_ref[dest, pl.ds(j * BLK, BLK), :] = total[block, :, :width].astype(out_ref.dtype)
            if with_degree:
                spread = jnp.where(eye, total[block, :, width:], 0.0)
                degree[j : j + 1, :] = jnp.sum(spread, axis=0, keepdims=True)
        if with_degree:
            out_ref[dest, pl.ds(DEV_BLOCKS * BLK, 16), :] = degree[...].astype(out_ref.dtype)


def product(plan, vals, hop, total, section, with_degree):
    pieces = [piece.reshape(-1, BLK, piece.shape[-1]) for piece in hop]
    blocks = sum(piece.shape[0] for piece in pieces)
    width = pieces[0].shape[2]
    wide = width + (BLK if with_degree else 0)
    out_shape = [pltpu.VMEM(total_shape, jnp.float32)]
    scratch = [
        pltpu.VMEM((blocks + 1, BLK, wide), jnp.bfloat16),
        pltpu.SemaphoreType.DMA((len(pieces),)),
    ]
    operands = [plan, vals, *pieces, total]
    in_specs = [smem_spec, vmem_spec] + [any_spec] * len(pieces) + [vmem_spec]
    aliases = {len(operands) - 1: 0}
    if section >= 1:
        rows = DEV_BLOCKS * BLK + (16 if with_degree else 0)
        out_shape.append(jax.ShapeDtypeStruct((DEST, rows, width), jnp.bfloat16))
        if with_degree:
            scratch.append(pltpu.VMEM((16, BLK), jnp.float32))
    flops = (6_000_000_000, 3_000_000_000, 3_000_000_000)[section]
    return pl.pallas_call(
        functools.partial(product_kernel, section, len(pieces)),
        out_shape=out_shape,
        in_specs=in_specs,
        out_specs=[vmem_spec] * len(out_shape),
        scratch_shapes=scratch,
        input_output_aliases=aliases,
        compiler_params=params(16),
        cost_estimate=pl.CostEstimate(flops=flops, bytes_accessed=1 << 20, transcendentals=0),
        name=("product_near", "product_send", "product_keep")[section],
    )(*operands)


def layer_product(plan, vals, total, hops, with_degree):
    (total,) = product(plan, vals, hops[0], total, 0, with_degree)
    total, send = product(plan, vals, hops[1], total, 1, with_degree)
    total, keep = product(plan, vals, hops[1], total, 2, with_degree)
    return send, keep


def row_mean(squares, count):
    return jnp.sum(squares.T, axis=0, keepdims=True) / count


def attr_kernel(own, attributes, w_attr, attr_bias, out_ref):
    for block in range(DEV_BLOCKS):
        rows = pl.ds(block * BLK, BLK)
        rebuilt = jnp.dot(own[rows, :], w_attr[...], preferred_element_type=jnp.float32)
        gap = rebuilt + attr_bias[...] - attributes[rows, :].astype(jnp.float32)
        out_ref[block : block + 1, :] = jnp.sqrt(row_mean(gap * gap, gap.shape[1]) + epsilon)


def attr_error(own, attributes, w_attr, attr_bias):
    return pl.pallas_call(
        attr_kernel,
        out_shape=jax.ShapeDtypeStruct((DEV_BLOCKS, BLK), jnp.float32),
        in_specs=[vmem_spec] * 4,
        out_specs=vmem_spec,
        compiler_params=params(16),
        cost_estimate=pl.CostEstimate(
            flops=500_000_000, bytes_accessed=1 << 19, transcendentals=0
        ),
        name="attr_error",
    )(own, attributes, w_attr, attr_bias)


def score_kernel(n_pieces, pair_ref, own, target, attr, *refs):
    pieces = refs[:n_pieces]
    out_ref, panel, sems = refs[n_pieces:]
    copies = start_panel(pieces, panel, sems)
    half_scale = 0.5 * own.shape[1] ** (-0.5)
    n_pair = pair_ref.shape[1]
    for copy in copies:
        copy.wait()
    for block in range(DEV_BLOCKS):
        rows = pl.ds(block * BLK, BLK)
        squares = jnp.zeros((BLK, BLK), jnp.float32)
        for pair in range(n_pair):
            logits = lax.dot_general(
                own[rows, :],
                panel[pair_ref[block, pair]],
                (((1,), (1,)), ((), ())),
                preferred_element_type=jnp.float32,
            )
            goal = target[rows, pl.ds(pair * BLK, BLK)].astype(jnp.float32)
            gap = 0.5 * jnp.tanh(logits * half_scale) + (0.5 - goal)
            squares = squares + gap * gap
        struct = jnp.sqrt(row_mean(squares, n_pair * BLK) + epsilon)
        mixed = mix_alpha * attr[block : block + 1, :] + (1.0 - mix_alpha) * struct
        out_ref[block : block + 1, :] = mixed


def score(hops, pairs, own, target, attr):
    pieces = [piece.reshape(-1, BLK, piece.shape[-1]) for hop in hops for piece in hop]
    out = pl.pallas_call(
        functools.partial(score_kernel, len(pieces)),
        out_shape=jax.ShapeDtypeStruct((DEV_BLOCKS, BLK), jnp.float32),
        in_specs=[smem_spec] + [vmem_spec] * 3 + [any_spec] * len(pieces),
        out_specs=vmem_spec,
        scratch_shapes=[
            pltpu.VMEM((N_ROW * DEV_BLOCKS, BLK, own.shape[1]), jnp.bfloat16),
            pltpu.SemaphoreType.DMA((len(pieces),)),
        ],
        compiler_params=params(16),
        name="score",
    )(pairs, own, target, attr, *pieces)
    return out.reshape(-1)


def relative_block(ids, row_at):
    owner = ids >> 2
    offset = (((owner >> 1) - (row_at >> 1)) & 3) * 2 + ((owner + row_at) & 1)
    hop = jnp.zeros_like(ids)
    place = jnp.zeros_like(ids)
    for at in range(N_ROW):
        hop = jnp.where(offset == at, HOP[at], hop)
        place = jnp.where(offset == at, PLACE[at], place)
    return hop, place * DEV_BLOCKS + (ids & 3)


def per_device(
    attributes,
    adj_values,
    adj_rows,
    adj_cols,
    adj_count,
    pair_ids,
    struct_target,
    w_first,
    w_rest,
    layer_bias,
    w_attr,
    attr_bias,
):
    hidden_size = w_rest.shape[1]
    row_at = lax.axis_index("row")
    col_at = lax.axis_index("col")
    vals, total, plan = begin(
        adj_values[0, 0], adj_rows[0, 0], adj_cols[0, 0], adj_count[0, 0], row_at, col_at
    )
    nodes_dev = attributes.shape[0]
    w_near, w_self = w_first[:, :hidden_size], w_first[:, hidden_size:]
    own_part = jnp.dot(attributes, w_self, preferred_element_type=jnp.float32)

    send, keep = layer_product(plan, vals, total, gather_row(attributes, True), True)
    summed = scatter_col(send, keep)
    degree = 1.0 + summed[nodes_dev : nodes_dev + DEV_BLOCKS].reshape(-1)
    row_scale = lax.rsqrt(degree)[:, None]
    aggregate = summed[:nodes_dev]
    coarse = lax.reduce_precision(aggregate, 8, 7)
    fine = (aggregate - coarse).astype(jnp.bfloat16)
    coarse = coarse.astype(jnp.bfloat16)
    mixed = jnp.dot(coarse, w_near, preferred_element_type=jnp.float32) + jnp.dot(
        fine, w_near, preferred_element_type=jnp.float32
    )
    hidden = jnp.tanh(row_scale * mixed + own_part).astype(jnp.bfloat16)

    features = jnp.dot(
        hidden, w_rest[0][:, :hidden_size], preferred_element_type=jnp.float32
    ).astype(jnp.bfloat16)
    hops = gather_row(features, True)
    own_part = (
        jnp.dot(hidden, w_rest[0][:, hidden_size:], preferred_element_type=jnp.float32)
        + layer_bias[0]
    )
    summed = scatter_col(*layer_product(plan, vals, cleared(keep), hops, False))
    hidden = jnp.tanh(row_scale * summed + own_part).astype(jnp.bfloat16)

    hop, place = relative_block(pair_ids, row_at)
    return score(
        gather_row(hidden, False),
        hop * (N_ROW // 2) * DEV_BLOCKS + place,
        hidden,
        struct_target.reshape(nodes_dev, -1),
        attr_error(hidden, attributes, w_attr, attr_bias[None, :]),
    )


def solution(mesh):
    return jax.shard_map(
        per_device,
        mesh=mesh,
        in_specs=(
            P(("row", "col"), None),
            P("row", "col", None, None, None),
            P("row", "col", None),
            P("row", "col", None),
            P("row", "col"),
            P(("row", "col"), None),
            P(("row", "col"), None, None),
            P(),
            P(),
            P(),
            P(),
            P(),
        ),
        out_specs=P(("row", "col")),
        check_vma=False,
    )
```

```python
import functools

import jax
import jax.numpy as jnp
from jax import lax
from jax.experimental import pallas as pl
from jax.experimental.pallas import tpu as pltpu
from jax.sharding import PartitionSpec as P

epsilon = 1e-06
mix_alpha = 0.8

BLK = 128
N_X, N_Y = 4, 4
N_ROW, N_COL = 8, 16
DEV_BLOCKS = 4
DEST = 8
HALF_BLOCKS = DEST * DEV_BLOCKS
HOP = (0, 0, 0, 1, 1, 1, 0, 1)
PLACE = (0, 1, 2, 1, 0, 3, 3, 2)
UNROLL = 20
TAKEN = 4
STEPS = 256
EMPTY = 31 * 512


def row_of(x, z_lo):
    return (x % N_X) * 2 + z_lo


def col_of(y, z_hi, core):
    return ((y % N_Y) * 2 + z_hi) * 2 + core


def shift_row(value, dx, dz):
    perm = [(row_of(x, z), row_of(x + dx, z ^ dz)) for x in range(N_X) for z in range(2)]
    return lax.ppermute(value, "row", perm)


def shift_col(value, dy, dz, dc):
    perm = [
        (col_of(y, z, c), col_of(y + dy, z ^ dz, c ^ dc))
        for y in range(N_Y)
        for z in range(2)
        for c in range(2)
    ]
    return lax.ppermute(value, "col", perm)


def gather_row(own, joined):
    from_left = shift_row(own, 1, 0)
    from_right = shift_row(own, -1, 0)
    from_z = shift_row(own, 0, 1)
    near = [own, from_z, from_right, from_left]
    left_z = shift_row(from_z, 1, 0)
    if joined:
        far_right_z = shift_row(jnp.concatenate([from_right, from_z]), -1, 0)
        far_z = shift_row(from_left, 1, 1)
        return near, [far_right_z, left_z, far_z]
    far_z = shift_row(from_left, 1, 1)
    far = shift_row(from_right, -1, 0)
    right_z = shift_row(from_right, 0, 1)
    return near, [far, right_z, left_z, far_z]


def add(*values):
    total = values[0].astype(jnp.float32)
    for value in values[1:]:
        total = total + value.astype(jnp.float32)
    return total


def scatter_col(send, keep):
    got = shift_col(send, 0, 0, 1)

    def pair(dy, dz, *more):
        at = dy * 2 + dz
        return add(keep[at], got[at], *more)

    def send(value, dy, dz):
        return shift_col(value.astype(jnp.bfloat16), dy, dz, 0)

    other = send(pair(0, 1), 0, 1)
    far_down = send(pair(2, 1), -1, 0)
    far_up = send(pair(2, 0), 1, 0)
    other, far_down, far_up = lax.optimization_barrier((other, far_down, far_up))
    direct_up = send(pair(1, 1), 1, 1)
    relay_down = send(pair(3, 1, far_down), -1, 1)
    relay_up = send(pair(1, 0, far_up), 1, 0)
    direct_down = send(pair(3, 0), -1, 0)
    return pair(0, 0, other, direct_up, relay_down, relay_up, direct_down)


def params(mib):
    return pltpu.CompilerParams(vmem_limit_bytes=mib * 1024 * 1024)


any_spec = pl.BlockSpec(memory_space=pl.ANY)
smem_spec = pl.BlockSpec(memory_space=pltpu.SMEM)
vmem_spec = pl.BlockSpec(memory_space=pltpu.VMEM)


def down(row):
    return jnp.broadcast_to(row.astype(jnp.float32), (BLK, row.shape[1])).T


def clear(total):
    @pl.loop(0, total.shape[0])
    def _(block):
        total[block] = jnp.zeros(total.shape[1:], jnp.float32)


def begin_kernel(place_ref, rows_in, cols_in, source, vals, total, plan, lists, sem, list_sem):
    copy = pltpu.make_async_copy(source, vals, sem)
    list_copies = [
        pltpu.make_async_copy(ids, lists.at[at], list_sem.at[at])
        for at, ids in enumerate((rows_in, cols_in))
    ]
    for list_copy in list_copies:
        list_copy.start()
    copy.start()
    for list_copy in list_copies:
        list_copy.wait()
    count, row_at, col_at = place_ref[0], place_ref[1], place_ref[2]
    y, z_hi, core = col_at >> 2, (col_at >> 1) & 1, col_at & 1
    rows = lists[0]
    capacity = rows.shape[1]
    slots = lax.broadcasted_iota(jnp.int32, rows.shape, 1)
    live = slots < count
    dest, j = rows >> 2, rows & 3
    dy = ((dest >> 2) - y) & 3
    dz = ((dest >> 1) + z_hi) & 1
    keep = 1 - ((dest + core) & 1)
    row = keep * HALF_BLOCKS + (dy * 2 + dz) * DEV_BLOCKS + j
    hop, col = relative_block(lists[1], row_at)
    section = jnp.where(hop == 1, 1 + keep, 0)
    key = jnp.where(live, section * (2 * HALF_BLOCKS) + row, 1024).astype(jnp.float32)
    parts = capacity // BLK
    square = (capacity, capacity)
    earlier = lax.broadcasted_iota(jnp.int32, square, 0) < lax.broadcasted_iota(jnp.int32, square, 1)

    def wide(column):
        return jnp.concatenate([column] * parts, axis=1)

    def tally(mask):
        return jnp.sum(jnp.where(mask, 1.0, 0.0), axis=0, keepdims=True)

    within = tally((wide(down(key)) == key) & earlier).astype(jnp.int32)
    opens = live & ((within & (TAKEN - 1)) == 0)
    opener = wide(down(jnp.where(opens, key, 2048.0)))
    least = (section * (2 * HALF_BLOCKS)).astype(jnp.float32)
    step = tally((opener >= least) & (opener < key)).astype(jnp.int32) + within // TAKEN
    lane = lax.broadcasted_iota(jnp.int32, (1, STEPS), 1)
    ends = jnp.zeros((1, 1), jnp.int32)
    begin = jnp.zeros(rows.shape, jnp.int32)
    bounds = jnp.zeros((1, STEPS), jnp.int32)
    for kind in range(3):
        begin = jnp.where(section == kind, ends, begin)
        mine = jnp.where(opens & (section == kind), 1.0, 0.0)
        number = jnp.sum(mine, axis=1, keepdims=True).astype(jnp.int32)
        ends = ends + (number + UNROLL - 1) // UNROLL * UNROLL
        bounds = jnp.where(lane == kind + 1, ends, bounds)
    spot = (begin + step) * TAKEN + (within & (TAKEN - 1))
    spot = down(jnp.where(live, spot, -1))
    word = down(slots + col * 512 + row * (512 * 32) - EMPTY)
    for side in range(TAKEN):
        for part in range(STEPS // BLK):
            here = lax.broadcasted_iota(jnp.int32, (1, BLK), 1) + part * BLK
            hit = spot == (here * TAKEN + side).astype(jnp.float32)
            found = jnp.sum(jnp.where(hit, word, 0.0), axis=0, keepdims=True)
            plan[side : side + 1, part * BLK : (part + 1) * BLK] = found.astype(jnp.int32) + EMPTY
    plan[TAKEN : TAKEN + 1, :] = bounds
    clear(total)
    copy.wait()


total_shape = (2 * HALF_BLOCKS, BLK, 2 * BLK)


def begin(vals, row_ids, col_ids, live_count, row_at, col_at):
    place = jnp.stack([live_count, row_at, col_at]).astype(jnp.int32)
    return pl.pallas_call(
        begin_kernel,
        out_shape=[
            pltpu.VMEM(vals.shape, vals.dtype),
            pltpu.VMEM(total_shape, jnp.float32),
            jax.ShapeDtypeStruct((TAKEN + 1, STEPS), jnp.int32),
        ],
        in_specs=[smem_spec] + [pl.BlockSpec(memory_space=pltpu.HBM)] * 3,
        out_specs=[vmem_spec] * 3,
        scratch_shapes=[
            pltpu.VMEM((2, 1, row_ids.shape[0]), jnp.int32),
            pltpu.SemaphoreType.DMA(()),
            pltpu.SemaphoreType.DMA((2,)),
        ],
        compiler_params=params(16),
        cost_estimate=pl.CostEstimate(flops=0, bytes_accessed=2 * vals.size, transcendentals=0),
        name="begin",
    )(
        place,
        pltpu.with_memory_space_constraint(row_ids[None, :], pltpu.HBM),
        pltpu.with_memory_space_constraint(col_ids[None, :], pltpu.HBM),
        pltpu.with_memory_space_constraint(vals, pltpu.HBM),
    )


def cleared(after):
    return pl.pallas_call(
        lambda after_ref, total: clear(total),
        out_shape=pltpu.VMEM(total_shape, jnp.float32),
        in_specs=[any_spec],
        out_specs=vmem_spec,
        compiler_params=params(16),
        cost_estimate=pl.CostEstimate(flops=0, bytes_accessed=1 << 21, transcendentals=0),
        name="cleared",
    )(after)


def start_panel(pieces, panel, sems):
    copies = []
    start = 0
    for index, piece in enumerate(pieces):
        where = panel.at[pl.ds(start, piece.shape[0]), :, pl.ds(0, piece.shape[2])]
        copies.append(pltpu.make_async_copy(piece, where, sems.at[index]))
        start += piece.shape[0]
    for copy in copies:
        copy.start()
    return copies


def product_kernel(section, with_degree, n_pieces, plan, vals, *refs):
    pieces = refs[:n_pieces]
    refs = refs[n_pieces + 1 :]
    last = section >= 1
    if section == 2:
        panel, refs = refs[0], refs[1:]
    total, refs = refs[0], refs[1:]
    if last:
        out_ref, refs = refs[0], refs[1:]
        width = out_ref.shape[2]
    if section < 2:
        panel, sems, refs = refs[0], refs[1], refs[2:]
        width = pieces[0].shape[2]
    zero_block = panel.shape[0] - 1

    if section < 2:
        copies = start_panel(pieces, panel, sems)
        panel[zero_block] = jnp.zeros(panel.shape[1:], panel.dtype)
        if with_degree:

            @pl.loop(0, zero_block)
            def _(block):
                panel[block, :, width:] = jnp.ones((BLK, panel.shape[2] - width), panel.dtype)

        for copy in copies:
            copy.wait()

    @pl.loop(plan[TAKEN, section], plan[TAKEN, section + 1], step=UNROLL)
    def _(group):
        for u in range(UNROLL):
            words = [plan[side, group + u] for side in range(TAKEN)]
            cols = [jnp.minimum((word >> 9) & 31, zero_block) for word in words]
            left = jnp.concatenate([vals[word & 511] for word in words], axis=1)
            right = jnp.concatenate([panel[col] for col in cols], axis=0)
            row = words[0] >> 14
            total[row] += jnp.dot(left, right, preferred_element_type=jnp.float32)

    if not last:
        return
    base = (section - 1) * HALF_BLOCKS
    if with_degree:
        degree = refs[0]
        degree[...] = jnp.zeros(degree.shape, jnp.float32)
        eye = lax.broadcasted_iota(jnp.int32, (BLK, BLK), 0) == lax.broadcasted_iota(
            jnp.int32, (BLK, BLK), 1
        )

    @pl.loop(0, DEST)
    def _(dest):
        for j in range(DEV_BLOCKS):
            block = base + dest * DEV_BLOCKS + j
            out_ref[dest, pl.ds(j * BLK, BLK), :] = total[block, :, :width].astype(out_ref.dtype)
            if with_degree:
                spread = jnp.where(eye, total[block, :, width:], 0.0)
                degree[j : j + 1, :] = jnp.sum(spread, axis=0, keepdims=True)
        if with_degree:
            out_ref[dest, pl.ds(DEV_BLOCKS * BLK, 16), :] = degree[...].astype(out_ref.dtype)


def product(plan, vals, hop, total, section, with_degree, panel=None):
    pieces = [piece.reshape(-1, BLK, piece.shape[-1]) for piece in hop]
    blocks = sum(piece.shape[0] for piece in pieces)
    width = pieces[0].shape[2]
    wide = width + (BLK if with_degree else 0)
    panel_shape = (blocks + 1, BLK, wide)
    sems = pltpu.SemaphoreType.DMA((len(pieces),))
    out_shape = [pltpu.VMEM(total_shape, jnp.float32)]
    scratch = []
    if section >= 1:
        rows = DEV_BLOCKS * BLK + (16 if with_degree else 0)
        out_shape.append(jax.ShapeDtypeStruct((DEST, rows, width), jnp.bfloat16))
    if section == 0:
        scratch += [pltpu.VMEM(panel_shape, jnp.bfloat16), sems]
    elif section == 1:
        out_shape.append(pltpu.VMEM(panel_shape, jnp.bfloat16))
        scratch.append(sems)
    else:
        pieces = []
    if section >= 1 and with_degree:
        scratch.append(pltpu.VMEM((16, BLK), jnp.float32))
    operands = [plan, vals, *pieces, total]
    aliases = {len(operands) - 1: 0}
    in_specs = [smem_spec, vmem_spec] + [any_spec] * len(pieces) + [vmem_spec]
    if section == 2:
        operands.append(panel)
        in_specs.append(vmem_spec)
    flops = (6_000_000_000, 3_000_000_000, 3_000_000_000)[section]
    return pl.pallas_call(
        functools.partial(product_kernel, section, with_degree, len(pieces)),
        out_shape=out_shape,
        in_specs=in_specs,
        out_specs=[vmem_spec] * len(out_shape),
        scratch_shapes=scratch,
        input_output_aliases=aliases,
        compiler_params=params(16),
        cost_estimate=pl.CostEstimate(flops=flops, bytes_accessed=1 << 20, transcendentals=0),
        name=("product_near", "product_send", "product_keep")[section],
    )(*operands)


def layer_product(plan, vals, total, hops, with_degree):
    (total,) = product(plan, vals, hops[0], total, 0, with_degree)
    total, send, panel = product(plan, vals, hops[1], total, 1, with_degree)
    total, keep = product(plan, vals, hops[1], total, 2, with_degree, panel)
    return send, keep


def row_mean(squares, count):
    return jnp.sum(squares.T, axis=0, keepdims=True) / count


def attr_kernel(own, attributes, w_attr, attr_bias, out_ref):
    for block in range(DEV_BLOCKS):
        rows = pl.ds(block * BLK, BLK)
        rebuilt = jnp.dot(own[rows, :], w_attr[...], preferred_element_type=jnp.float32)
        gap = rebuilt + attr_bias[...] - attributes[rows, :].astype(jnp.float32)
        out_ref[block : block + 1, :] = jnp.sqrt(row_mean(gap * gap, gap.shape[1]) + epsilon)


def attr_error(own, attributes, w_attr, attr_bias):
    return pl.pallas_call(
        attr_kernel,
        out_shape=jax.ShapeDtypeStruct((DEV_BLOCKS, BLK), jnp.float32),
        in_specs=[vmem_spec] * 4,
        out_specs=vmem_spec,
        compiler_params=params(16),
        cost_estimate=pl.CostEstimate(
            flops=500_000_000, bytes_accessed=1 << 19, transcendentals=0
        ),
        name="attr_error",
    )(own, attributes, w_attr, attr_bias)


def score_kernel(n_pieces, pair_ref, own, target, attr, *refs):
    pieces = refs[:n_pieces]
    out_ref, panel, sems = refs[n_pieces:]
    copies = start_panel(pieces, panel, sems)
    half_scale = 0.5 * own.shape[1] ** (-0.5)
    n_pair = pair_ref.shape[1]
    for copy in copies:
        copy.wait()
    for block in range(DEV_BLOCKS):
        rows = pl.ds(block * BLK, BLK)
        squares = jnp.zeros((BLK, BLK), jnp.float32)
        for pair in range(n_pair):
            logits = lax.dot_general(
                own[rows, :],
                panel[pair_ref[block, pair]],
                (((1,), (1,)), ((), ())),
                preferred_element_type=jnp.float32,
            )
            goal = target[rows, pl.ds(pair * BLK, BLK)].astype(jnp.float32)
            gap = 0.5 * jnp.tanh(logits * half_scale) + (0.5 - goal)
            squares = squares + gap * gap
        struct = jnp.sqrt(row_mean(squares, n_pair * BLK) + epsilon)
        mixed = mix_alpha * attr[block : block + 1, :] + (1.0 - mix_alpha) * struct
        out_ref[block : block + 1, :] = mixed


def score(hops, pairs, own, target, attr):
    pieces = [piece.reshape(-1, BLK, piece.shape[-1]) for hop in hops for piece in hop]
    out = pl.pallas_call(
        functools.partial(score_kernel, len(pieces)),
        out_shape=jax.ShapeDtypeStruct((DEV_BLOCKS, BLK), jnp.float32),
        in_specs=[smem_spec] + [vmem_spec] * 3 + [any_spec] * len(pieces),
        out_specs=vmem_spec,
        scratch_shapes=[
            pltpu.VMEM((N_ROW * DEV_BLOCKS, BLK, own.shape[1]), jnp.bfloat16),
            pltpu.SemaphoreType.DMA((len(pieces),)),
        ],
        compiler_params=params(16),
        name="score",
    )(pairs, own, target, attr, *pieces)
    return out.reshape(-1)


def relative_block(ids, row_at):
    owner = ids >> 2
    offset = (((owner >> 1) - (row_at >> 1)) & 3) * 2 + ((owner + row_at) & 1)
    hop = jnp.zeros_like(ids)
    place = jnp.zeros_like(ids)
    for at in range(N_ROW):
        hop = jnp.where(offset == at, HOP[at], hop)
        place = jnp.where(offset == at, PLACE[at], place)
    return hop, place * DEV_BLOCKS + (ids & 3)


def per_device(
    attributes,
    adj_values,
    adj_rows,
    adj_cols,
    adj_count,
    pair_ids,
    struct_target,
    w_first,
    w_rest,
    layer_bias,
    w_attr,
    attr_bias,
):
    hidden_size = w_rest.shape[1]
    row_at = lax.axis_index("row")
    col_at = lax.axis_index("col")
    vals, total, plan = begin(
        adj_values[0, 0], adj_rows[0, 0], adj_cols[0, 0], adj_count[0, 0], row_at, col_at
    )
    nodes_dev = attributes.shape[0]
    w_near, w_self = w_first[:, :hidden_size], w_first[:, hidden_size:]
    own_part = jnp.dot(attributes, w_self, preferred_element_type=jnp.float32)

    send, keep = layer_product(plan, vals, total, gather_row(attributes, True), True)
    summed = scatter_col(send, keep)
    degree = 1.0 + summed[nodes_dev : nodes_dev + DEV_BLOCKS].reshape(-1)
    row_scale = lax.rsqrt(degree)[:, None]
    aggregate = summed[:nodes_dev]
    coarse = lax.reduce_precision(aggregate, 8, 7)
    fine = (aggregate - coarse).astype(jnp.bfloat16)
    coarse = coarse.astype(jnp.bfloat16)
    mixed = jnp.dot(coarse, w_near, preferred_element_type=jnp.float32) + jnp.dot(
        fine, w_near, preferred_element_type=jnp.float32
    )
    hidden = jnp.tanh(row_scale * mixed + own_part).astype(jnp.bfloat16)

    features = jnp.dot(
        hidden, w_rest[0][:, :hidden_size], preferred_element_type=jnp.float32
    ).astype(jnp.bfloat16)
    hops = gather_row(features, True)
    own_part = (
        jnp.dot(hidden, w_rest[0][:, hidden_size:], preferred_element_type=jnp.float32)
        + layer_bias[0]
    )
    summed = scatter_col(*layer_product(plan, vals, cleared(keep), hops, False))
    hidden = jnp.tanh(row_scale * summed + own_part).astype(jnp.bfloat16)

    hop, place = relative_block(pair_ids, row_at)
    return score(
        gather_row(hidden, False),
        hop * (N_ROW // 2) * DEV_BLOCKS + place,
        hidden,
        struct_target.reshape(nodes_dev, -1),
        attr_error(hidden, attributes, w_attr, attr_bias[None, :]),
    )


def solution(mesh):
    return jax.shard_map(
        per_device,
        mesh=mesh,
        in_specs=(
            P(("row", "col"), None),
            P("row", "col", None, None, None),
            P("row", "col", None),
            P("row", "col", None),
            P("row", "col"),
            P(("row", "col"), None),
            P(("row", "col"), None, None),
            P(),
            P(),
            P(),
            P(),
            P(),
        ),
        out_specs=P(("row", "col")),
        check_vma=False,
    )
```

```python
import functools

import jax
import jax.numpy as jnp
from jax import lax
from jax.experimental import pallas as pl
from jax.experimental.pallas import tpu as pltpu
from jax.sharding import PartitionSpec as P

epsilon = 1e-06
mix_alpha = 0.8

BLK = 128
N_X, N_Y = 4, 4
N_ROW, N_COL = 8, 16
DEV_BLOCKS = 4
DEST = 8
HALF_BLOCKS = DEST * DEV_BLOCKS
HOP = (0, 0, 0, 1, 1, 1, 0, 1)
PLACE = (0, 1, 2, 1, 0, 3, 3, 2)
UNROLL = (26, 20, 20)
TAKEN = 4
STEPS = 256
EMPTY = 31 * 512


def row_of(x, z_lo):
    return (x % N_X) * 2 + z_lo


def col_of(y, z_hi, core):
    return ((y % N_Y) * 2 + z_hi) * 2 + core


def shift_row(value, dx, dz):
    perm = [(row_of(x, z), row_of(x + dx, z ^ dz)) for x in range(N_X) for z in range(2)]
    return lax.ppermute(value, "row", perm)


def shift_col(value, dy, dz, dc):
    perm = [
        (col_of(y, z, c), col_of(y + dy, z ^ dz, c ^ dc))
        for y in range(N_Y)
        for z in range(2)
        for c in range(2)
    ]
    return lax.ppermute(value, "col", perm)


def gather_row(own, joined):
    from_left = shift_row(own, 1, 0)
    from_right = shift_row(own, -1, 0)
    from_z = shift_row(own, 0, 1)
    near = [own, from_z, from_right, from_left]
    left_z = shift_row(from_z, 1, 0)
    if joined:
        far_right_z = shift_row(jnp.concatenate([from_right, from_z]), -1, 0)
        far_z = shift_row(from_left, 1, 1)
        return near, [far_right_z, left_z, far_z]
    far_z = shift_row(from_left, 1, 1)
    far = shift_row(from_right, -1, 0)
    right_z = shift_row(from_right, 0, 1)
    return near, [far, right_z, left_z, far_z]


def add(*values):
    total = values[0].astype(jnp.float32)
    for value in values[1:]:
        total = total + value.astype(jnp.float32)
    return total


def scatter_col(send, keep):
    got = shift_col(send, 0, 0, 1)

    def pair(dy, dz, *more):
        at = dy * 2 + dz
        return add(keep[at], got[at], *more)

    def send(value, dy, dz):
        return shift_col(value.astype(jnp.bfloat16), dy, dz, 0)

    other = send(pair(0, 1), 0, 1)
    far_down = send(pair(2, 1), -1, 0)
    far_up = send(pair(2, 0), 1, 0)
    other, far_down, far_up = lax.optimization_barrier((other, far_down, far_up))
    direct_up = send(pair(1, 1), 1, 1)
    relay_down = send(pair(3, 1, far_down), -1, 1)
    relay_up = send(pair(1, 0, far_up), 1, 0)
    direct_down = send(pair(3, 0), -1, 0)
    return pair(0, 0, other, direct_up, relay_down, relay_up, direct_down)


def params(mib):
    return pltpu.CompilerParams(vmem_limit_bytes=mib * 1024 * 1024)


any_spec = pl.BlockSpec(memory_space=pl.ANY)
smem_spec = pl.BlockSpec(memory_space=pltpu.SMEM)
vmem_spec = pl.BlockSpec(memory_space=pltpu.VMEM)


def down(row):
    return jnp.broadcast_to(row.astype(jnp.float32), (BLK, row.shape[1])).T


def clear(total):
    @pl.loop(0, total.shape[0])
    def _(block):
        total[block] = jnp.zeros(total.shape[1:], jnp.float32)


def begin_kernel(place_ref, rows_in, cols_in, source, vals, total, plan, lists, sem, list_sem):
    copy = pltpu.make_async_copy(source, vals, sem)
    list_copies = [
        pltpu.make_async_copy(ids, lists.at[at], list_sem.at[at])
        for at, ids in enumerate((rows_in, cols_in))
    ]
    for list_copy in list_copies:
        list_copy.start()
    copy.start()
    for list_copy in list_copies:
        list_copy.wait()
    count, row_at, col_at = place_ref[0], place_ref[1], place_ref[2]
    y, z_hi, core = col_at >> 2, (col_at >> 1) & 1, col_at & 1
    rows = lists[0]
    capacity = rows.shape[1]
    slots = lax.broadcasted_iota(jnp.int32, rows.shape, 1)
    live = slots < count
    dest, j = rows >> 2, rows & 3
    dy = ((dest >> 2) - y) & 3
    dz = ((dest >> 1) + z_hi) & 1
    keep = 1 - ((dest + core) & 1)
    row = keep * HALF_BLOCKS + (dy * 2 + dz) * DEV_BLOCKS + j
    hop, col = relative_block(lists[1], row_at)
    section = jnp.where(hop == 1, 1 + keep, 0)
    key = jnp.where(live, section * (2 * HALF_BLOCKS) + row, 1024).astype(jnp.float32)
    parts = capacity // BLK
    square = (capacity, capacity)
    earlier = lax.broadcasted_iota(jnp.int32, square, 0) < lax.broadcasted_iota(jnp.int32, square, 1)

    def wide(column):
        return jnp.concatenate([column] * parts, axis=1)

    def tally(mask):
        return jnp.sum(jnp.where(mask, 1.0, 0.0), axis=0, keepdims=True)

    within = tally((wide(down(key)) == key) & earlier).astype(jnp.int32)
    opens = live & ((within & (TAKEN - 1)) == 0)
    opener = wide(down(jnp.where(opens, key, 2048.0)))
    least = (section * (2 * HALF_BLOCKS)).astype(jnp.float32)
    step = tally((opener >= least) & (opener < key)).astype(jnp.int32) + within // TAKEN
    lane = lax.broadcasted_iota(jnp.int32, (1, STEPS), 1)
    ends = jnp.zeros((1, 1), jnp.int32)
    begin = jnp.zeros(rows.shape, jnp.int32)
    bounds = jnp.zeros((1, STEPS), jnp.int32)
    for kind in range(3):
        begin = jnp.where(section == kind, ends, begin)
        mine = jnp.where(opens & (section == kind), 1.0, 0.0)
        number = jnp.sum(mine, axis=1, keepdims=True).astype(jnp.int32)
        group = UNROLL[kind]
        ends = ends + (number + group - 1) // group * group
        bounds = jnp.where(lane == kind + 1, ends, bounds)
    spot = (begin + step) * TAKEN + (within & (TAKEN - 1))
    spot = down(jnp.where(live, spot, -1))
    word = down(slots + col * 512 + row * (512 * 32) - EMPTY)
    for side in range(TAKEN):
        for part in range(STEPS // BLK):
            here = lax.broadcasted_iota(jnp.int32, (1, BLK), 1) + part * BLK
            hit = spot == (here * TAKEN + side).astype(jnp.float32)
            found = jnp.sum(jnp.where(hit, word, 0.0), axis=0, keepdims=True)
            plan[side : side + 1, part * BLK : (part + 1) * BLK] = found.astype(jnp.int32) + EMPTY
    plan[TAKEN : TAKEN + 1, :] = bounds
    clear(total)
    copy.wait()


total_shape = (2 * HALF_BLOCKS, BLK, 2 * BLK)


def begin(vals, row_ids, col_ids, live_count, row_at, col_at):
    place = jnp.stack([live_count, row_at, col_at]).astype(jnp.int32)
    return pl.pallas_call(
        begin_kernel,
        out_shape=[
            pltpu.VMEM(vals.shape, vals.dtype),
            pltpu.VMEM(total_shape, jnp.float32),
            jax.ShapeDtypeStruct((TAKEN + 1, STEPS), jnp.int32),
        ],
        in_specs=[smem_spec] + [pl.BlockSpec(memory_space=pltpu.HBM)] * 3,
        out_specs=[vmem_spec] * 3,
        scratch_shapes=[
            pltpu.VMEM((2, 1, row_ids.shape[0]), jnp.int32),
            pltpu.SemaphoreType.DMA(()),
            pltpu.SemaphoreType.DMA((2,)),
        ],
        compiler_params=params(16),
        cost_estimate=pl.CostEstimate(flops=0, bytes_accessed=2 * vals.size, transcendentals=0),
        name="begin",
    )(
        place,
        pltpu.with_memory_space_constraint(row_ids[None, :], pltpu.HBM),
        pltpu.with_memory_space_constraint(col_ids[None, :], pltpu.HBM),
        pltpu.with_memory_space_constraint(vals, pltpu.HBM),
    )


def cleared(after):
    return pl.pallas_call(
        lambda after_ref, total: clear(total),
        out_shape=pltpu.VMEM(total_shape, jnp.float32),
        in_specs=[any_spec],
        out_specs=vmem_spec,
        compiler_params=params(16),
        cost_estimate=pl.CostEstimate(flops=0, bytes_accessed=1 << 21, transcendentals=0),
        name="cleared",
    )(after)


def start_panel(pieces, panel, sems):
    copies = []
    start = 0
    for index, piece in enumerate(pieces):
        where = panel.at[pl.ds(start, piece.shape[0]), :, pl.ds(0, piece.shape[2])]
        copies.append(pltpu.make_async_copy(piece, where, sems.at[index]))
        start += piece.shape[0]
    for copy in copies:
        copy.start()
    return copies


def product_kernel(section, with_degree, n_pieces, plan, vals, *refs):
    pieces = refs[:n_pieces]
    refs = refs[n_pieces + 1 :]
    last = section >= 1
    if section == 2:
        panel, refs = refs[0], refs[1:]
    total, refs = refs[0], refs[1:]
    if last:
        out_ref, refs = refs[0], refs[1:]
        width = out_ref.shape[2]
    if section < 2:
        panel, sems, refs = refs[0], refs[1], refs[2:]
        width = pieces[0].shape[2]
    zero_block = panel.shape[0] - 1

    if section < 2:
        copies = start_panel(pieces, panel, sems)
        panel[zero_block] = jnp.zeros(panel.shape[1:], panel.dtype)
        if with_degree:

            @pl.loop(0, zero_block)
            def _(block):
                panel[block, :, width:] = jnp.ones((BLK, panel.shape[2] - width), panel.dtype)

        for copy in copies:
            copy.wait()

    @pl.loop(plan[TAKEN, section], plan[TAKEN, section + 1], step=UNROLL[section])
    def _(group):
        for u in range(UNROLL[section]):
            words = [plan[side, group + u] for side in range(TAKEN)]
            cols = [jnp.minimum((word >> 9) & 31, zero_block) for word in words]
            left = jnp.concatenate([vals[word & 511] for word in words], axis=1)
            right = jnp.concatenate([panel[col] for col in cols], axis=0)
            row = words[0] >> 14
            total[row] += jnp.dot(left, right, preferred_element_type=jnp.float32)

    if not last:
        return
    base = (section - 1) * HALF_BLOCKS
    if with_degree:
        degree = refs[0]
        degree[...] = jnp.zeros(degree.shape, jnp.float32)
        eye = lax.broadcasted_iota(jnp.int32, (BLK, BLK), 0) == lax.broadcasted_iota(
            jnp.int32, (BLK, BLK), 1
        )

    @pl.loop(0, DEST)
    def _(dest):
        for j in range(DEV_BLOCKS):
            block = base + dest * DEV_BLOCKS + j
            out_ref[dest, pl.ds(j * BLK, BLK), :] = total[block, :, :width].astype(out_ref.dtype)
            if with_degree:
                spread = jnp.where(eye, total[block, :, width:], 0.0)
                degree[j : j + 1, :] = jnp.sum(spread, axis=0, keepdims=True)
        if with_degree:
            out_ref[dest, pl.ds(DEV_BLOCKS * BLK, 16), :] = degree[...].astype(out_ref.dtype)


def product(plan, vals, hop, total, section, with_degree, panel=None):
    pieces = [piece.reshape(-1, BLK, piece.shape[-1]) for piece in hop]
    blocks = sum(piece.shape[0] for piece in pieces)
    width = pieces[0].shape[2]
    wide = width + (BLK if with_degree else 0)
    panel_shape = (blocks + 1, BLK, wide)
    sems = pltpu.SemaphoreType.DMA((len(pieces),))
    out_shape = [pltpu.VMEM(total_shape, jnp.float32)]
    scratch = []
    if section >= 1:
        rows = DEV_BLOCKS * BLK + (16 if with_degree else 0)
        out_shape.append(jax.ShapeDtypeStruct((DEST, rows, width), jnp.bfloat16))
    if section == 0:
        scratch += [pltpu.VMEM(panel_shape, jnp.bfloat16), sems]
    elif section == 1:
        out_shape.append(pltpu.VMEM(panel_shape, jnp.bfloat16))
        scratch.append(sems)
    else:
        pieces = []
    if section >= 1 and with_degree:
        scratch.append(pltpu.VMEM((16, BLK), jnp.float32))
    operands = [plan, vals, *pieces, total]
    aliases = {len(operands) - 1: 0}
    in_specs = [smem_spec, vmem_spec] + [any_spec] * len(pieces) + [vmem_spec]
    if section == 2:
        operands.append(panel)
        in_specs.append(vmem_spec)
    flops = (6_000_000_000, 3_000_000_000, 3_000_000_000)[section]
    return pl.pallas_call(
        functools.partial(product_kernel, section, with_degree, len(pieces)),
        out_shape=out_shape,
        in_specs=in_specs,
        out_specs=[vmem_spec] * len(out_shape),
        scratch_shapes=scratch,
        input_output_aliases=aliases,
        compiler_params=params(16),
        cost_estimate=pl.CostEstimate(flops=flops, bytes_accessed=1 << 20, transcendentals=0),
        name=("product_near", "product_send", "product_keep")[section],
    )(*operands)


def layer_product(plan, vals, total, hops, with_degree):
    (total,) = product(plan, vals, hops[0], total, 0, with_degree)
    total, send, panel = product(plan, vals, hops[1], total, 1, with_degree)
    total, keep = product(plan, vals, hops[1], total, 2, with_degree, panel)
    return send, keep


def row_mean(squares, count):
    return jnp.sum(squares.T, axis=0, keepdims=True) / count


def attr_kernel(own, attributes, w_attr, attr_bias, out_ref):
    for block in range(DEV_BLOCKS):
        rows = pl.ds(block * BLK, BLK)
        rebuilt = jnp.dot(own[rows, :], w_attr[...], preferred_element_type=jnp.float32)
        gap = rebuilt + attr_bias[...] - attributes[rows, :].astype(jnp.float32)
        out_ref[block : block + 1, :] = jnp.sqrt(row_mean(gap * gap, gap.shape[1]) + epsilon)


def attr_error(own, attributes, w_attr, attr_bias):
    return pl.pallas_call(
        attr_kernel,
        out_shape=jax.ShapeDtypeStruct((DEV_BLOCKS, BLK), jnp.float32),
        in_specs=[vmem_spec] * 4,
        out_specs=vmem_spec,
        compiler_params=params(16),
        cost_estimate=pl.CostEstimate(
            flops=500_000_000, bytes_accessed=1 << 19, transcendentals=0
        ),
        name="attr_error",
    )(own, attributes, w_attr, attr_bias)


def score_kernel(n_pieces, pair_ref, own, target, attr, *refs):
    pieces = refs[:n_pieces]
    out_ref, panel, sems = refs[n_pieces:]
    copies = start_panel(pieces, panel, sems)
    half_scale = 0.5 * own.shape[1] ** (-0.5)
    n_pair = pair_ref.shape[1]
    for copy in copies:
        copy.wait()
    for block in range(DEV_BLOCKS):
        rows = pl.ds(block * BLK, BLK)
        squares = jnp.zeros((BLK, BLK), jnp.float32)
        for pair in range(n_pair):
            logits = lax.dot_general(
                own[rows, :],
                panel[pair_ref[block, pair]],
                (((1,), (1,)), ((), ())),
                preferred_element_type=jnp.float32,
            )
            goal = target[rows, pl.ds(pair * BLK, BLK)].astype(jnp.float32)
            gap = 0.5 * jnp.tanh(logits * half_scale) + (0.5 - goal)
            squares = squares + gap * gap
        struct = jnp.sqrt(row_mean(squares, n_pair * BLK) + epsilon)
        mixed = mix_alpha * attr[block : block + 1, :] + (1.0 - mix_alpha) * struct
        out_ref[block : block + 1, :] = mixed


def score(hops, pairs, own, target, attr):
    pieces = [piece.reshape(-1, BLK, piece.shape[-1]) for hop in hops for piece in hop]
    out = pl.pallas_call(
        functools.partial(score_kernel, len(pieces)),
        out_shape=jax.ShapeDtypeStruct((DEV_BLOCKS, BLK), jnp.float32),
        in_specs=[smem_spec] + [vmem_spec] * 3 + [any_spec] * len(pieces),
        out_specs=vmem_spec,
        scratch_shapes=[
            pltpu.VMEM((N_ROW * DEV_BLOCKS, BLK, own.shape[1]), jnp.bfloat16),
            pltpu.SemaphoreType.DMA((len(pieces),)),
        ],
        compiler_params=params(16),
        name="score",
    )(pairs, own, target, attr, *pieces)
    return out.reshape(-1)


def relative_block(ids, row_at):
    owner = ids >> 2
    offset = (((owner >> 1) - (row_at >> 1)) & 3) * 2 + ((owner + row_at) & 1)
    hop = jnp.zeros_like(ids)
    place = jnp.zeros_like(ids)
    for at in range(N_ROW):
        hop = jnp.where(offset == at, HOP[at], hop)
        place = jnp.where(offset == at, PLACE[at], place)
    return hop, place * DEV_BLOCKS + (ids & 3)


def per_device(
    attributes,
    adj_values,
    adj_rows,
    adj_cols,
    adj_count,
    pair_ids,
    struct_target,
    w_first,
    w_rest,
    layer_bias,
    w_attr,
    attr_bias,
):
    hidden_size = w_rest.shape[1]
    row_at = lax.axis_index("row")
    col_at = lax.axis_index("col")
    vals, total, plan = begin(
        adj_values[0, 0], adj_rows[0, 0], adj_cols[0, 0], adj_count[0, 0], row_at, col_at
    )
    nodes_dev = attributes.shape[0]
    w_near, w_self = w_first[:, :hidden_size], w_first[:, hidden_size:]
    own_part = jnp.dot(attributes, w_self, preferred_element_type=jnp.float32)

    send, keep = layer_product(plan, vals, total, gather_row(attributes, True), True)
    summed = scatter_col(send, keep)
    degree = 1.0 + summed[nodes_dev : nodes_dev + DEV_BLOCKS].reshape(-1)
    row_scale = lax.rsqrt(degree)[:, None]
    aggregate = summed[:nodes_dev]
    coarse = lax.reduce_precision(aggregate, 8, 7)
    fine = (aggregate - coarse).astype(jnp.bfloat16)
    coarse = coarse.astype(jnp.bfloat16)
    mixed = jnp.dot(coarse, w_near, preferred_element_type=jnp.float32) + jnp.dot(
        fine, w_near, preferred_element_type=jnp.float32
    )
    hidden = jnp.tanh(row_scale * mixed + own_part).astype(jnp.bfloat16)

    features = jnp.dot(
        hidden, w_rest[0][:, :hidden_size], preferred_element_type=jnp.float32
    ).astype(jnp.bfloat16)
    hops = gather_row(features, True)
    own_part = (
        jnp.dot(hidden, w_rest[0][:, hidden_size:], preferred_element_type=jnp.float32)
        + layer_bias[0]
    )
    summed = scatter_col(*layer_product(plan, vals, cleared(keep), hops, False))
    hidden = jnp.tanh(row_scale * summed + own_part).astype(jnp.bfloat16)

    hop, place = relative_block(pair_ids, row_at)
    return score(
        gather_row(hidden, False),
        hop * (N_ROW // 2) * DEV_BLOCKS + place,
        hidden,
        struct_target.reshape(nodes_dev, -1),
        attr_error(hidden, attributes, w_attr, attr_bias[None, :]),
    )


def solution(mesh):
    return jax.shard_map(
        per_device,
        mesh=mesh,
        in_specs=(
            P(("row", "col"), None),
            P("row", "col", None, None, None),
            P("row", "col", None),
            P("row", "col", None),
            P("row", "col"),
            P(("row", "col"), None),
            P(("row", "col"), None, None),
            P(),
            P(),
            P(),
            P(),
            P(),
        ),
        out_specs=P(("row", "col")),
        check_vma=False,
    )
```
